512 devices in a mesh: slab: 2 (over core), row: 16 (over z), col: 16 (over x, y).
Axes of the slice: x: 4, y: 4, z: 16, core: 2. Of those that a mesh axis runs over, the one named last changes fastest.
Arguments:
- video: bfloat16 [8, 128, 49152], P('slab', 'row', 'col'), may hold values from -40 to 40
- cache_in: bfloat16 [2, 128, 49152], P(None, 'row', 'col'), may hold values from -4 to 4
- cache_mid: bfloat16 [2, 128, 49152], P(None, 'row', 'col'), may hold values from -4 to 4
- gain_in: float32 [192], replicated, may hold values from 0.1 to 1.9
- gain_mid: float32 [192], replicated, may hold values from 0.1 to 1.9
- conv_in: bfloat16 [3, 3, 110592], replicated, may hold values from -0.078125 to 0.078125
- bias_in: float32 [192], replicated, may hold values from -3 to 3
- conv_mid: bfloat16 [3, 3, 110592], replicated, may hold values from -0.078125 to 0.078125
- bias_mid: float32 [192], replicated, may hold values from -3 to 3
Outputs:
- decoded: bfloat16 [8, 128, 49152], P('slab', 'row', 'col')
The draws below stay inside these ranges and needn't reach their ends.
All inputs are finite; a program needn't handle non-finite values.
Results may differ from the reference program's by a relative error of at most 0.0022.
Values may be sent and summed in bfloat16 or wider, within the bound.
A program may use at most 64 MiB of HBM per device.

```python
import jax
import jax.numpy as jnp
from jax import lax

CHAN = 192
FRAMES = 8
HEIGHT = 128
WIDTH = 256


def draw_video(key, part):
    key = jax.random.fold_in(key, 11)
    key_base, key_chan, key_pixel = jax.random.split(key, 3)
    shape = (FRAMES, HEIGHT, WIDTH, CHAN)
    base = jnp.clip(jax.random.normal(key_base, shape, jnp.float32), -3.9, 3.9)
    chan_scale = jnp.exp(jax.random.uniform(key_chan, (CHAN,), jnp.float32, -1.15, 1.15))
    pixel_scale = jnp.exp(jax.random.uniform(key_pixel, (FRAMES, HEIGHT, WIDTH, 1), jnp.float32, -1.15, 1.15))
    values = base * chan_scale * pixel_scale
    return values.reshape(FRAMES, HEIGHT, WIDTH * CHAN).astype(jnp.bfloat16)


def level_of(own_key, shape, pieces, least, high):
    def one(dim, parts):
        draws = jax.random.uniform(jax.random.fold_in(jax.random.fold_in(own_key, 6), dim), (parts,), jnp.float32, least / len(pieces), high / len(pieces))
        return jnp.repeat(jnp.exp(draws), shape[dim] // parts).reshape((-1,) + (1,) * (len(shape) - dim - 1))

    loudness = one(*pieces[0])
    for cut in pieces[1:]:
        loudness = loudness * one(*cut)
    return loudness


def centred(own_key, dims, spread, limit, pieces=(), dtype=jnp.bfloat16):
    level = level_of(own_key, dims, pieces, -0.22, 0.18) if pieces else 1.0
    drawn = jax.random.normal(own_key, dims, jnp.float32) * spread * level
    return jnp.minimum(jnp.maximum(drawn, -limit), limit).astype(dtype)


def setup_inputs(seed: int = 0) -> dict:
    streams_of = jax.random.split(jax.random.key(seed), 10)
    video = draw_video(jax.random.fold_in(streams_of[9], 71), 0)
    cache_in = centred(streams_of[1], (2, HEIGHT, WIDTH * CHAN), 0.6, 4.0, ((1, 16), (2, 16)))
    cache_mid = centred(streams_of[2], (2, HEIGHT, WIDTH * CHAN), 0.6, 4.0, ((1, 16), (2, 16)))
    gain_in = jnp.clip(1.0 + 0.18 * jax.random.normal(streams_of[3], (CHAN,), jnp.float32), 0.1, 1.9)
    gain_mid = jnp.clip(1.0 + 0.18 * jax.random.normal(streams_of[4], (CHAN,), jnp.float32), 0.1, 1.9)
    conv_in = centred(streams_of[5], (3, 3, 3 * CHAN * CHAN), (27 * CHAN) ** -0.5, 0.078125)
    bias_in = centred(streams_of[6], (CHAN,), 0.5, 3.0, (), jnp.float32)
    conv_mid = centred(streams_of[7], (3, 3, 3 * CHAN * CHAN), (27 * CHAN) ** -0.5, 0.078125)
    bias_mid = centred(streams_of[8], (CHAN,), 0.5, 3.0, (), jnp.float32)
    return dict(video=video, cache_in=cache_in, cache_mid=cache_mid, gain_in=gain_in, gain_mid=gain_mid, conv_in=conv_in, bias_in=bias_in, conv_mid=conv_mid, bias_mid=bias_mid)


def activate(values, gain):
    values = values.astype(jnp.float32)
    mean_sq = lax.optimization_barrier(jnp.mean(values * values, axis=-1, keepdims=True))
    return jax.nn.silu(values * lax.rsqrt(mean_sq + 1e-06) * gain)

def convolve(padded, kernel, bias):
    frames = padded.shape[0] - 2
    height = padded.shape[1] - 2
    width = padded.shape[2] - 2
    chans = padded.shape[3]
    total = jnp.zeros((frames * height * width, bias.shape[0]), jnp.float32)
    for step_t in range(3):
        for step_h in range(3):
            rows = padded[step_t:step_t + frames, step_h:step_h + height]
            stacked = jnp.concatenate([rows[:, :, q:q + width] for q in range(3)], axis=-1)
            stacked = stacked.reshape(-1, 3 * chans).astype(jnp.float32)
            taps = kernel[step_t, step_h].reshape(3 * chans, -1).astype(jnp.float32)
            total = total + jnp.dot(stacked, taps, preferred_element_type=jnp.float32)
    return total.reshape(frames, height, width, -1) + bias

def reference(video, cache_in, cache_mid, gain_in, gain_mid, conv_in, bias_in, conv_mid, bias_mid):
    chans = gain_in.shape[0]
    video = video.reshape(FRAMES, HEIGHT, WIDTH, chans)
    cache_in = cache_in.reshape(2, HEIGHT, WIDTH, chans)
    cache_mid = cache_mid.reshape(2, HEIGHT, WIDTH, chans)
    first = activate(video, gain_in).astype(jnp.bfloat16)
    seq_in = jnp.concatenate([cache_in, first], axis=0)
    padded = jnp.pad(seq_in, ((0, 0), (1, 1), (1, 1), (0, 0)))
    middle = []
    for frame in range(FRAMES):
        hidden = convolve(padded[frame:frame + 3], conv_in, bias_in)
        middle.append(activate(hidden, gain_mid).astype(jnp.bfloat16))
    seq_mid = jnp.concatenate([cache_mid] + middle, axis=0)
    padded_mid = jnp.pad(seq_mid, ((0, 0), (1, 1), (1, 1), (0, 0)))
    outputs = []
    for frame in range(FRAMES):
        branch = convolve(padded_mid[frame:frame + 3], conv_mid, bias_mid)
        outputs.append((video[frame:frame + 1].astype(jnp.float32) + branch).astype(jnp.bfloat16))
    return jnp.concatenate(outputs, axis=0).reshape(FRAMES, HEIGHT, WIDTH * chans)
```

```python
import functools

import jax
import jax.numpy as jnp
from jax import lax
from jax.experimental import pallas as pl
from jax.experimental.pallas import tpu as pltpu
from jax.sharding import PartitionSpec as P

F32 = jnp.float32
BF16 = jnp.bfloat16
CHAN = 192
PITCH = 20
ROWS_IN, COLS_IN = 12, 20
ROWS_MID, COLS_MID = 10, 18
EARLY_IN = 30
EARLY_MID = 26
AROUND = [(-1, 0), (1, 0), (0, -1), (0, 1), (-1, -1), (-1, 1), (1, -1), (1, 1)]


def low_lanes(shape):
    return lax.broadcasted_iota(jnp.int32, shape, len(shape) - 1) < 64


def low_subs(shape):
    return lax.broadcasted_iota(jnp.int32, shape, len(shape) - 2) < 4


def swap(x):
    return pltpu.roll(x, 64, 1)


def act(a, b, gain_a, gain_b, lanes):
    square = a * a + jnp.where(lanes, b * b, 0.0)
    mean = jnp.sum(square, axis=1, keepdims=True) * (1.0 / CHAN)
    scale = lax.rsqrt(mean + 1e-6)
    ua, ub = a * scale * gain_a, b * scale * gain_b
    return ua / (1.0 + jnp.exp(-ua)), ub / (1.0 + jnp.exp(-ub))


def order_channels(order):
    c = lax.broadcasted_iota(jnp.int32, (256, 256), 0)
    o = lax.broadcasted_iota(jnp.int32, (256, 256), 1)
    o = jnp.where(o < CHAN, o, o - 64)
    r = o & 15
    source = (o - r) + jnp.where(r < 8, 2 * r, 2 * r - 15)
    order[...] = jnp.where(c == source, 1.0, 0.0).astype(BF16)


def lay_out_weights(raw, wide, out):
    per = wide.shape[0] // 24
    lanes = low_lanes((8, 128))
    flat = wide.reshape(wide.shape[0] * 8, 128)
    out[:, 13 * 128 : 13 * 128 + 64, :] = jnp.zeros((3, 64, 256), BF16)

    def step(n, _):
        a, part = n // (36 // per), n % (36 // per)
        for u in range(per):
            g = part * per + u
            wide[pl.ds(u * 24, 24), 0:3, :] = raw[a, pl.ds(g * 24, 24)].astype(F32)
            q, group = g // 12, g % 12
            for p in range(3):
                first = flat[pl.ds(u * 192 + p, 8, stride=24)]
                both = flat[pl.ds(u * 192 + 8 + p, 8, stride=24)]
                second = swap(flat[pl.ds(u * 192 + 16 + p, 8, stride=24)])
                odd = jnp.where(lanes, swap(both), second)
                row_a = (p * 3 + q) * 128 + 16 * group
                row_b = (9 + q) * 128 + 64 * p if p < 2 else 12 * 128 + 64 * q + jnp.where(q == 2, 64, 0)
                row = jnp.where(group < 8, row_a, row_b + 16 * (group - 8))
                row = pl.multiple_of(row, 16)
                out[a, pl.ds(row, 16), 0:128] = jnp.concatenate([first, odd], 0).astype(BF16)
                out[a, pl.ds(row, 16), 128:256] = jnp.concatenate([both, second], 0).astype(BF16)
        return 0

    lax.fori_loop(0, 3 * 36 // per, step, 0)


def pack_early(sa, sb, early, groups):
    lanes = low_lanes((16, 128))

    def frames(s, g):
        start = pl.multiple_of(g * 64, 64)
        return jnp.concatenate([s[pl.ds(start + 4, 8, stride=8)], s[pl.ds(start + 5, 8, stride=8)]], 0)

    def step(g, _):
        early[g] = frames(sa, g).astype(BF16)
        early[g + groups // 2] = frames(sa, g + groups // 2).astype(BF16)
        early[g + groups] = jnp.where(lanes, frames(sb, g), frames(sb, g + groups // 2)).astype(BF16)
        return 0

    lax.fori_loop(0, groups // 2, step, 0)


def unpack_early(sa, sb, early, groups):
    lanes = low_lanes((16, 128))

    def put(s, g, x):
        start = pl.multiple_of(g * 64, 64)
        s[pl.ds(start, 8, stride=8)] = x[0:8]
        s[pl.ds(start + 1, 8, stride=8)] = x[8:16]

    def step(g, _):
        put(sa, g, early[g].astype(F32))
        put(sa, g + groups // 2, early[g + groups // 2].astype(F32))
        b = early[g + groups].astype(F32)
        other = swap(b)
        put(sb, g, jnp.where(lanes, b, other))
        put(sb, g + groups // 2, jnp.where(lanes, other, b))
        return 0

    lax.fori_loop(0, groups // 2, step, 0)


def gather_taps(sa, sb, ta, tb, zp, zq, a, up, left, rows, cols):
    subs = low_subs((8, 128))
    lanes = low_lanes((16, 128))

    def pair(s, start, i, j):
        first = s[pl.ds(start + (i * PITCH + j) * 8 + a, 8), :]
        second = s[pl.ds(start + (i * PITCH + j + left) * 8 + a - 4, 8), :]
        return jnp.where(subs, first, second)

    def quad(s, start, j):
        return jnp.concatenate([pair(s, start, 0, j), pair(s, start, up, j)], 0).astype(BF16)

    def step(i, _):
        start = pl.multiple_of(i * (PITCH * 8), 8)
        for j in range(cols):
            ta[a, i, j] = quad(sa, start, j)
            tb[a, i, j] = quad(sb, start, j)
        return 0

    lax.fori_loop(0, rows, step, 0)

    def merge(i, _):
        for j in range(cols):
            zp[a, i, j] = jnp.where(lanes, tb[a, i, j], tb[a, i + 1, j])
        for j in range(cols - 1):
            zq[a, i, j] = jnp.where(lanes, tb[a, i + 2, j], tb[a, i + 2, j + 1])
        return 0

    lax.fori_loop(0, rows - 2, merge, 0)


def tap_columns(ta, zp, zq, a, rows, cols):
    parts = [ta[a, p : p + rows, q : q + cols] for p in range(3) for q in range(3)]
    parts += [zp[a, 0:rows, q : q + cols] for q in range(3)]
    parts += [zq[a, 0:rows, q : q + cols] for q in range(2)]
    return [x.reshape(rows * cols * 16, 128) for x in parts]


def convolve(ta, zp, zq, weights, times, rows, cols):
    columns = sum([tap_columns(ta, zp, zq, a, rows, cols) for a in times], [])
    weight = weights[times[0] : times[-1] + 1].reshape(len(times) * 14 * 128, 256)
    return jnp.dot(jnp.concatenate(columns, 1), weight, preferred_element_type=F32)


def kernel(sizes, video_hbm, cin_hbm, cmid_hbm, gain_in, gain_mid, win_hbm, bias_in, wmid_hbm, bias_mid, out,
           video, cin, cmid, raw_in, raw_mid, w_in, w_mid, wide, natural, mixed, order, sa, sb, s2a, s2b,
           units, early_in, early_mid, ta, tb, zp, zq, total,
           load_sem, send_sem, recv_sem, early_send, early_recv):
    n_row, n_col = sizes
    slab, row, col = lax.axis_index("slab"), lax.axis_index("row"), lax.axis_index("col")
    loads = [pltpu.make_async_copy(src, dst, load_sem.at[n]) for n, (src, dst) in enumerate(
        [(video_hbm, video), (cin_hbm, cin), (cmid_hbm, cmid), (win_hbm, raw_in), (wmid_hbm, raw_mid)])]
    for load in loads:
        load.start()

    def neighbour(dr, dc):
        return (slab, lax.rem(row + dr + n_row, n_row), lax.rem(col + dc + n_col, n_col))

    barrier = pltpu.get_barrier_semaphore()
    for dr, dc in AROUND:
        pl.semaphore_signal(barrier, inc=1, device_id=neighbour(dr, dc), device_id_type=pl.DeviceIdType.MESH)
    pl.semaphore_signal(barrier, inc=1, device_id=(1 - slab, row, col), device_id_type=pl.DeviceIdType.MESH)

    lanes8, lanes16 = low_lanes((8, 128)), low_lanes((16, 128))
    zero = jnp.zeros((1, 64), F32)

    def halves(ref):
        return ref[0:1, 0:128], jnp.concatenate([ref[0:1, 128:192], zero], 1)

    order_channels(order)
    for load in loads[:3]:
        load.wait()

    def spread(t, _):
        for f in range(2):
            natural[t, f] = cin[f, t].astype(F32)
            natural[t, 6 + f] = cmid[f, t].astype(F32)
        for f in range(4):
            natural[t, 2 + f] = video[f, t].astype(F32)
        return 0

    lax.fori_loop(0, 24, spread, 0, unroll=4)
    flat = natural.reshape(24 * 64, 128)
    gain_a, gain_b = halves(gain_in)
    sub = lax.broadcasted_iota(jnp.int32, (8, 128), 0)
    moving = (sub >= 2) & (sub < 6)

    def activate_row(i, _):
        for j in range(8):
            t0, t1, t2 = (flat[pl.ds((3 * j + k) * 64 + i, 8, stride=8)] for k in range(3))
            t1s, t2s = swap(t1), swap(t2)
            pixels = [(t0, t1), (jnp.where(lanes8, t1s, t2s), t2s)]
            done = []
            for a, b in pixels:
                ya, yb = act(a, b, gain_a, gain_b, lanes8)
                done.append((jnp.where(moving, ya, a), jnp.where(moving, yb, b)))
            start = pl.multiple_of(i * 128 + j * 16, 16)
            mixed[pl.ds(start, 16), 0:128] = jnp.concatenate([done[0][0], done[1][0]], 0).astype(BF16)
            mixed[pl.ds(start, 16), 128:256] = jnp.concatenate([done[0][1], done[1][1]], 0).astype(BF16)
        return 0

    lax.fori_loop(0, 8, activate_row, 0)

    def place_rows(u, _):
        start = pl.multiple_of(u * 256, 256)
        ordered = jnp.dot(mixed[pl.ds(start, 256), :], order[...], preferred_element_type=F32)
        for r in range(2):
            at = pl.multiple_of(((2 * u + r + 2) * PITCH + 2) * 8, 8)
            sa[pl.ds(at, 128), :] = ordered[r * 128 : r * 128 + 128, 0:128]
            sb[pl.ds(at, 128), :] = ordered[r * 128 : r * 128 + 128, 128:256]
        small = ordered.astype(BF16)
        for v in range(8):
            top, low = small[v * 16 : v * 16 + 16], small[128 + v * 16 : 128 + v * 16 + 16]
            units[u + 1, v + 1, 0] = top[:, 0:128]
            units[u + 1, v + 1, 1] = low[:, 0:128]
            units[u + 1, v + 1, 2] = jnp.where(lanes16, top[:, 128:256], low[:, 128:256])
        return 0

    lax.fori_loop(0, 4, place_rows, 0)

    pl.semaphore_wait(barrier, 9)

    def span(step, count, away):
        if step == 0:
            return pl.ds(1, count)
        near, far = (1, count + 1) if step < 0 else (count, 0)
        return pl.ds(far if away else near, 1)

    copies = []
    for n, (dr, dc) in enumerate(AROUND):
        copies.append(pltpu.make_async_remote_copy(
            src_ref=units.at[span(dr, 4, False), span(dc, 8, False)],
            dst_ref=units.at[span(dr, 4, True), span(dc, 8, True)],
            send_sem=send_sem.at[n], recv_sem=recv_sem.at[n],
            device_id=neighbour(dr, dc), device_id_type=pl.DeviceIdType.MESH))
    for copy in copies:
        copy.start()

    loads[3].wait()
    lay_out_weights(raw_in, wide, w_in)
    loads[4].wait()
    lay_out_weights(raw_mid, wide, w_mid)

    for copy in copies:
        copy.wait()

    inside_up, inside_down = (row > 0).astype(F32), (row < n_row - 1).astype(F32)
    inside_left, inside_right = (col > 0).astype(F32), (col < n_col - 1).astype(F32)

    def place_unit(u, v, keep):
        at = pl.multiple_of((2 * u * PITCH + 2 * v) * 8, 8)
        sa[pl.ds(at, 16), :] = units[u, v, 0].astype(F32) * keep
        sa[pl.ds(at + PITCH * 8, 16), :] = units[u, v, 1].astype(F32) * keep
        b = units[u, v, 2].astype(F32) * keep
        other = swap(b)
        sb[pl.ds(at, 16), :] = jnp.where(lanes16, b, other)
        sb[pl.ds(at + PITCH * 8, 16), :] = jnp.where(lanes16, other, b)

    for v in range(10):
        side = inside_left if v == 0 else inside_right if v == 9 else 1.0
        place_unit(0, v, inside_up * side)
        place_unit(5, v, inside_down * side)
    for u in range(1, 5):
        place_unit(u, 0, inside_left)
        place_unit(u, 9, inside_right)

    early_copies = [pltpu.make_async_remote_copy(
        src_ref=e, dst_ref=e, send_sem=early_send.at[n], recv_sem=early_recv.at[n],
        device_id=(1 - slab, row, col), device_id_type=pl.DeviceIdType.MESH) for n, e in enumerate((early_in, early_mid))]

    @pl.when(slab == 0)
    def _():
        pack_early(sa, sb, early_in, EARLY_IN)
        early_copies[0].start()

    def place_cache(i, _):
        source = pl.multiple_of(((i + 1) * PITCH + 1) * 8, 8)
        at = pl.multiple_of(i * (PITCH * 8), 8)
        for s, s2 in ((sa, s2a), (sb, s2b)):
            s2[pl.ds(at, COLS_MID * 8), :] = s[pl.ds(source + 6, COLS_MID * 8), :]
        return 0

    lax.fori_loop(0, ROWS_MID, place_cache, 0)

    gather_taps(sa, sb, ta, tb, zp, zq, 2, 5, 9, 7, 11)
    total[...] = convolve(ta, zp, zq, w_in, [2], 5, 9)

    @pl.when(slab == 1)
    def _():
        early_copies[0].wait_recv()
        unpack_early(sa, sb, early_in, EARLY_IN)

    for a in range(2):
        gather_taps(sa, sb, ta, tb, zp, zq, a, 5, 9, 7, 11)
    total[...] += convolve(ta, zp, zq, w_in, [0, 1], 5, 9)

    bias_a, bias_b = halves(bias_in)
    gain_a, gain_b = halves(gain_mid)
    subs16 = lax.broadcasted_iota(jnp.int32, (16, 128), 0)
    left_subs = (subs16 & 4) == 0

    def activate_middle(i, _):
        keep_rows = jnp.where(
            subs16 < 8,
            jnp.where(i == 0, inside_up, 1.0),
            jnp.where(i == 4, inside_down, 1.0))
        for j in range(9):
            start = pl.multiple_of(i * 144 + j * 16, 16)
            a = total[pl.ds(start, 16), 0:128] + bias_a
            b = total[pl.ds(start, 16), 128:256] + bias_b
            ya, yb = act(a, b, gain_a, gain_b, lanes16)
            keep = keep_rows
            if j == 0:
                keep = jnp.where(left_subs, keep * inside_left, keep)
            if j == 8:
                keep = jnp.where(left_subs, keep, keep * inside_right)
            mixed[pl.ds(start, 16), 0:128] = (ya * keep).astype(BF16)
            mixed[pl.ds(start, 16), 128:256] = (yb * keep).astype(BF16)
        return 0

    lax.fori_loop(0, 5, activate_middle, 0)

    def place_middle(i, _):
        start = pl.multiple_of(i * 144, 16)
        ordered = jnp.dot(mixed[pl.ds(start, 144), :], order[...], preferred_element_type=F32)
        at = pl.multiple_of(i * (PITCH * 8), 8)
        for j in range(9):
            for n, step in enumerate((0, 9, 5 * PITCH, 5 * PITCH + 9)):
                y = ordered[j * 16 + 4 * n : j * 16 + 4 * n + 4]
                s2a[pl.ds(at + (j + step) * 8 + 2, 4), :] = y[:, 0:128]
                s2b[pl.ds(at + (j + step) * 8 + 2, 4), :] = y[:, 128:256]
        return 0

    lax.fori_loop(0, 5, place_middle, 0)

    @pl.when(slab == 0)
    def _():
        pack_early(s2a, s2b, early_mid, EARLY_MID)
        early_copies[1].start()

    gather_taps(s2a, s2b, ta, tb, zp, zq, 2, 4, 8, 6, 10)
    total[0:512] = convolve(ta, zp, zq, w_mid, [2], 4, 8)

    @pl.when(slab == 1)
    def _():
        early_copies[1].wait_recv()
        unpack_early(s2a, s2b, early_mid, EARLY_MID)

    for a in range(2):
        gather_taps(s2a, s2b, ta, tb, zp, zq, a, 4, 8, 6, 10)
    total[0:512] += convolve(ta, zp, zq, w_mid, [0, 1], 4, 8)

    bias_a, bias_b = halves(bias_mid)

    def restore(i, _):
        for j in range(4):
            start = pl.multiple_of(i * 128 + j * 32, 32)
            for h in range(2):
                even, odd = start + 8 * h, start + 16 + 8 * h
                ae = total[pl.ds(even, 8), 0:128] + bias_a
                be = total[pl.ds(even, 8), 128:256] + bias_b
                ao = swap(total[pl.ds(odd, 8), 0:128] + bias_a)
                bo = swap(total[pl.ds(odd, 8), 128:256] + bias_b)
                natural[3 * j, i + 4 * h] = ae
                natural[3 * j + 1, i + 4 * h] = jnp.where(lanes8, be, ao)
                natural[3 * j + 2, i + 4 * h] = jnp.where(lanes8, ao, bo)
        return 0

    lax.fori_loop(0, 4, restore, 0)

    def finish(t, _):
        start = pl.multiple_of(t * 64, 64)
        for h in range(2):
            for f in range(4):
                branch = flat[pl.ds(start + 4 * h + f, 8, stride=8)]
                out[f, t + 12 * h] = (video[f, t + 12 * h].astype(F32) + branch).astype(BF16)
        return 0

    lax.fori_loop(0, 12, finish, 0, unroll=4)

    @pl.when(slab == 0)
    def _():
        early_copies[0].wait_send()
        early_copies[1].wait_send()


def body(sizes, video, cache_in, cache_mid, gain_in, gain_mid, conv_in, bias_in, conv_mid, bias_mid):
    def tiles(x):
        return x.reshape(x.shape[0], 8, 24, 128).transpose(0, 2, 1, 3)

    def taps(x):
        return x.reshape(3, 3, 864, 128).transpose(0, 2, 1, 3)

    def line(x):
        return x.reshape(1, CHAN)

    hbm, vmem = pl.BlockSpec(memory_space=pl.ANY), pl.BlockSpec(memory_space=pltpu.VMEM)
    scratch = [
        pltpu.VMEM((4, 24, 8, 128), BF16),
        pltpu.VMEM((2, 24, 8, 128), BF16),
        pltpu.VMEM((2, 24, 8, 128), BF16),
        pltpu.VMEM((3, 864, 3, 128), BF16),
        pltpu.VMEM((3, 864, 3, 128), BF16),
        pltpu.VMEM((3, 14 * 128, 256), BF16),
        pltpu.VMEM((3, 14 * 128, 256), BF16),
        pltpu.VMEM((4 * 24, 8, 128), F32),
        pltpu.VMEM((24, 8, 8, 128), F32),
        pltpu.VMEM((1024, 256), BF16),
        pltpu.VMEM((256, 256), BF16),
        pltpu.VMEM((ROWS_IN * PITCH * 8, 128), F32),
        pltpu.VMEM((ROWS_IN * PITCH * 8, 128), F32),
        pltpu.VMEM((EARLY_MID * 64, 128), F32),
        pltpu.VMEM((EARLY_MID * 64, 128), F32),
        pltpu.VMEM((6, 10, 3, 16, 128), BF16),
        pltpu.VMEM((EARLY_IN * 3 // 2, 16, 128), BF16),
        pltpu.VMEM((EARLY_MID * 3 // 2, 16, 128), BF16),
        pltpu.VMEM((3, 7, 11, 16, 128), BF16),
        pltpu.VMEM((3, 7, 11, 16, 128), BF16),
        pltpu.VMEM((3, 5, 11, 16, 128), BF16),
        pltpu.VMEM((3, 5, 10, 16, 128), BF16),
        pltpu.VMEM((720, 256), F32),
        pltpu.SemaphoreType.DMA((5,)),
        pltpu.SemaphoreType.DMA((8,)),
        pltpu.SemaphoreType.DMA((8,)),
        pltpu.SemaphoreType.DMA((2,)),
        pltpu.SemaphoreType.DMA((2,)),
    ]
    result = pl.pallas_call(
        functools.partial(kernel, sizes),
        out_shape=jax.ShapeDtypeStruct((4, 24, 8, 128), BF16),
        in_specs=[hbm, hbm, hbm, vmem, vmem, hbm, vmem, hbm, vmem],
        out_specs=vmem,
        scratch_shapes=scratch,
        compiler_params=pltpu.CompilerParams(
            collective_id=0, has_side_effects=True, vmem_limit_bytes=48 << 20),
        cost_estimate=pl.CostEstimate(flops=3_000_000_000, bytes_accessed=6_000_000, transcendentals=300_000),
    )(tiles(video), tiles(cache_in), tiles(cache_mid), line(gain_in), line(gain_mid),
      taps(conv_in), line(bias_in), taps(conv_mid), line(bias_mid))
    return result.transpose(0, 2, 1, 3).reshape(video.shape)


def solution(mesh):
    tile = P("slab", "row", "col")
    cache = P(None, "row", "col")
    sizes = (mesh.shape["row"], mesh.shape["col"])
    return jax.shard_map(
        functools.partial(body, sizes), mesh=mesh,
        in_specs=(tile, cache, cache, P(), P(), P(), P(), P(), P()),
        out_specs=tile, check_vma=False)
```

```python
import functools

import jax
import jax.numpy as jnp
from jax import lax
from jax.experimental import pallas as pl
from jax.experimental.pallas import tpu as pltpu
from jax.sharding import PartitionSpec as P

F32 = jnp.float32
BF16 = jnp.bfloat16
CHAN = 192
HALF = 20
LINE = 2 * HALF
PAD = 3
IMAGE = 13 * LINE
MIDDLE = 5 * LINE
AROUND = [(-1, 0), (1, 0), (0, -1), (0, 1), (-1, -1), (-1, 1), (1, -1), (1, 1)]


def low_lanes(shape):
    return lax.broadcasted_iota(jnp.int32, shape, len(shape) - 1) < 64


def swap(x):
    return pltpu.roll(x, 64, 1)


def act(a, b, gain_a, gain_b, lanes):
    square = a * a + jnp.where(lanes, b * b, 0.0)
    mean = jnp.sum(square, axis=1, keepdims=True) * (1.0 / CHAN)
    scale = lax.rsqrt(mean + 1e-6)
    ua, ub = a * scale * gain_a, b * scale * gain_b
    return ua / (1.0 + jnp.exp(-ua)), ub / (1.0 + jnp.exp(-ub))


def order_channels(order):
    c = lax.broadcasted_iota(jnp.int32, (256, 256), 0)
    o = lax.broadcasted_iota(jnp.int32, (256, 256), 1)
    o = jnp.where(o < CHAN, o, o - 64)
    r = o & 15
    source = (o - r) + jnp.where(r < 8, 2 * r, 2 * r - 15)
    order[...] = jnp.where(c == source, 1.0, 0.0).astype(BF16)


def lay_out_weights(raw, wide, out):
    per = wide.shape[0] // 24
    lanes = low_lanes((8, 128))
    flat = wide.reshape(wide.shape[0] * 8, 128)
    out[:, 13 * 128 : 13 * 128 + 64, :] = jnp.zeros((3, 64, 256), BF16)

    def step(n, _):
        a, part = n // (36 // per), n % (36 // per)
        for u in range(per):
            g = part * per + u
            wide[pl.ds(u * 24, 24), 0:3, :] = raw[a, pl.ds(g * 24, 24)].astype(F32)
            q, group = g // 12, g % 12
            for p in range(3):
                first = flat[pl.ds(u * 192 + p, 8, stride=24)]
                both = flat[pl.ds(u * 192 + 8 + p, 8, stride=24)]
                second = swap(flat[pl.ds(u * 192 + 16 + p, 8, stride=24)])
                odd = jnp.where(lanes, swap(both), second)
                row_a = (p * 3 + q) * 128 + 16 * group
                row_b = (9 + q) * 128 + 64 * p if p < 2 else 12 * 128 + 64 * q + jnp.where(q == 2, 64, 0)
                row = jnp.where(group < 8, row_a, row_b + 16 * (group - 8))
                row = pl.multiple_of(row, 16)
                out[a, pl.ds(row, 16), 0:128] = jnp.concatenate([first, odd], 0).astype(BF16)
                out[a, pl.ds(row, 16), 128:256] = jnp.concatenate([both, second], 0).astype(BF16)
        return 0

    lax.fori_loop(0, 3 * 36 // per, step, 0)


def split_columns(t0, t1, t2, lanes):
    t1s, t2s = swap(t1), swap(t2)
    return [(t0, t1), (jnp.where(lanes, t1s, t2s), t2s)]


def gather_taps(sa, sb, ta, tb, start_of, step, apart, pairs, rows, cols):
    size = start_of(1, 0, 0) - start_of(0, 0, 0)

    def tile(s, at):
        first = s[pl.ds(at, 8, stride=step), :]
        second = s[pl.ds(at + apart * size, 8, stride=step), :]
        return jnp.concatenate([first, second], 0).astype(BF16)

    def body(n, _):
        g, i = n // rows, n % rows
        for j in range(cols):
            at = start_of(g, i, j)
            ta[g, i, j] = tile(sa, at)
            tb[g, i, j] = tile(sb, at)
        return 0

    lax.fori_loop(0, pairs * rows, body, 0)


def merge_taps(tb, zp, zq, pairs, rows, cols):
    lanes = low_lanes((16, 128))

    def body(n, _):
        g, i = n // rows, n % rows
        for j in range(cols):
            zp[g, i, j] = jnp.where(lanes, tb[g, i, j], tb[g, i + 1, j])
        for j in range(cols - 1):
            zq[g, i, j] = jnp.where(lanes, tb[g, i + 2, j], tb[g, i + 2, j + 1])
        return 0

    lax.fori_loop(0, pairs * rows, body, 0)


def convolve(ta, zp, zq, weights, pairs, rows, cols):
    columns = []
    for a in range(3):
        g = slice(a, a + pairs)
        columns += [ta[g, p : p + rows, q : q + cols] for p in range(3) for q in range(3)]
        columns += [zp[g, :, q : q + cols] for q in range(3)]
        columns += [zq[g, :, q : q + cols] for q in range(2)]
    columns = [x.reshape(pairs * rows * cols * 16, 128) for x in columns]
    weight = weights[...].reshape(3 * 14 * 128, 256)
    return jnp.dot(jnp.concatenate(columns, 1), weight, preferred_element_type=F32)


def kernel(sizes, video_hbm, cin_hbm, cmid_hbm, gin_hbm, gmid_hbm, win_hbm, bin_hbm, wmid_hbm, bmid_hbm, out,
           gain_in, gain_mid, bias_in, bias_mid, video, cin, cmid, raw_in, raw_mid, w_in, w_mid, wide, mixed, order,
           oa, ob, corner, sa, sb, ma, mb, tile, side, angle, got_tile, got_row, got_side, got_angle,
           ta, tb, zp, zq, ua, ub, vp, vq, total_a, total_b,
           load_sem, send_sem, recv_sem, tile_sem):
    n_row, n_col = sizes
    slab, row, col = lax.axis_index("slab"), lax.axis_index("row"), lax.axis_index("col")
    loads = [pltpu.make_async_copy(src, dst, load_sem.at[n]) for n, (src, dst) in enumerate(
        [(video_hbm, video), (cin_hbm, cin), (cmid_hbm, cmid), (gin_hbm, gain_in), (gmid_hbm, gain_mid),
         (bin_hbm, bias_in), (bmid_hbm, bias_mid), (win_hbm, raw_in), (wmid_hbm, raw_mid)])]
    for load in loads:
        load.start()

    up, down, left, right = row > 0, row < n_row - 1, col > 0, col < n_col - 1
    there = [up, down, left, right, up & left, up & right, down & left, down & right]

    def device(s, dr, dc):
        return (s, lax.rem(row + dr + n_row, n_row), lax.rem(col + dc + n_col, n_col))

    barrier = pltpu.get_barrier_semaphore()
    for s in range(2):
        for (dr, dc), has in zip(AROUND, there):
            @pl.when(has)
            def _():
                pl.semaphore_signal(barrier, inc=1, device_id=device(s, dr, dc), device_id_type=pl.DeviceIdType.MESH)
    pl.semaphore_signal(barrier, inc=1, device_id=(1 - slab, row, col), device_id_type=pl.DeviceIdType.MESH)
    n_up_down, n_sides = up.astype(jnp.int32) + down.astype(jnp.int32), left.astype(jnp.int32) + right.astype(jnp.int32)
    greetings = 2 * (n_up_down + n_sides + n_up_down * n_sides) + 1

    lanes8, lanes16 = low_lanes((8, 128)), low_lanes((16, 128))
    zero = jnp.zeros((1, 64), F32)

    def halves(ref):
        return ref[0:1, 0:128], jnp.concatenate([ref[0:1, 128:192], zero], 1)

    order_channels(order)
    for load in loads[:7]:
        load.wait()

    def columns_of(ref, f, j):
        return split_columns(*(ref[f, 3 * j + k].astype(F32) for k in range(3)), lanes8)

    def put_mixed(f, j, pixels):
        start = pl.multiple_of(f * 128 + j * 16, 16)
        mixed[pl.ds(start, 16), 0:128] = jnp.concatenate([pixels[0][0], pixels[1][0]], 0).astype(BF16)
        mixed[pl.ds(start, 16), 128:256] = jnp.concatenate([pixels[0][1], pixels[1][1]], 0).astype(BF16)

    gain_a, gain_b = halves(gain_in)

    def activate_frame(n, _):
        f = n // 2
        for k in range(4):
            j = (n % 2) * 4 + k
            put_mixed(f, j, [act(a, b, gain_a, gain_b, lanes8) for a, b in columns_of(video, f, j)])
        return 0

    def mix_caches(j, _):
        for f in range(2):
            put_mixed(f, j, columns_of(cmid, f, j))
            put_mixed(2 + f, j, columns_of(cin, f, j))
        return 0

    def reorder():
        ordered = jnp.dot(mixed[0:512], order[...], preferred_element_type=F32)
        oa[...] = ordered[:, 0:128]
        ob[...] = ordered[:, 128:256]

    def line_of(o, f, i):
        return [o[pl.ds(f * 128 + h * 64 + i, 8, stride=8), :] for h in range(2)]

    def pack(k):
        def two_rows(n, _):
            f, u = n // 4, n % 4
            for r in range(2):
                tile[k, f, u, r] = jnp.concatenate(line_of(oa, f, 2 * u + r), 0).astype(BF16)
            b = [jnp.concatenate(line_of(ob, f, 2 * u + r), 0) for r in range(2)]
            tile[k, f, u, 2] = jnp.where(lanes16, b[0], b[1]).astype(BF16)
            return 0

        lax.fori_loop(0, 16, two_rows, 0, unroll=4)
        for v, j in enumerate((0, 14)):
            for f in range(4):
                side[k, v, f // 2, f % 2] = oa[pl.ds((f * 16 + j) * 8, 16), :].astype(BF16)
            for f in range(0, 4, 2):
                b = [ob[pl.ds(((f + e) * 16 + j) * 8, 16), :] for e in range(2)]
                side[k, v, f // 2, 2] = jnp.where(lanes16, b[0], b[1]).astype(BF16)
        for n, (i0, j0) in enumerate(((0, 0), (0, 14), (6, 0), (6, 14))):
            for h, o in enumerate((oa, ob)):
                for x in range(4):
                    at = (j0 + x % 2) * 8 + i0 + x // 2
                    corner[2 * n + h, 4 * x : 4 * x + 4, :] = o[pl.ds(at, 4, stride=128), :]
        for n in range(4):
            for h in range(2):
                angle[k, n, h] = corner[2 * n + h].astype(BF16)

    def messages(k, s, slot):
        sources = [tile.at[k, :, 0], tile.at[k, :, 3], side.at[k, 0], side.at[k, 1]] + [angle.at[k, n] for n in range(4)]
        targets = [got_row.at[slot, 1], got_row.at[slot, 0], got_side.at[slot, 1], got_side.at[slot, 0]]
        targets += [got_angle.at[slot, 3 - n] for n in range(4)]
        return [pltpu.make_async_remote_copy(
            src_ref=src, dst_ref=dst, send_sem=send_sem.at[slot, n], recv_sem=recv_sem.at[slot, n],
            device_id=device(s, dr, dc), device_id_type=pl.DeviceIdType.MESH)
            for n, (src, dst, (dr, dc)) in enumerate(zip(sources, targets, AROUND))]

    def each(copies, method, condition=None):
        exist = [there[n] for n in (1, 0, 3, 2, 7, 6, 5, 4)] if method == "wait_recv" else there
        for copy, has in zip(copies, exist):
            @pl.when(has if condition is None else has & condition)
            def _():
                getattr(copy, method)()

    own = messages(0, slab, 1)
    early_frames = messages(0, 1, 0)
    early_caches = messages(1, 0, 0)
    to_partner = pltpu.make_async_remote_copy(
        src_ref=tile.at[0], dst_ref=got_tile, send_sem=tile_sem.at[0], recv_sem=tile_sem.at[1],
        device_id=(1 - slab, row, col), device_id_type=pl.DeviceIdType.MESH)

    def place_tile(f0):
        def one(f, i, line, r):
            at = ((f0 + f) * 13 + line + PAD) * LINE + r * HALF + 2
            for o, s in ((oa, sa), (ob, sb)):
                for h, x in enumerate(line_of(o, f, i)):
                    s[pl.ds(at + 8 * h, 8), :] = x

        def frame(f, _):
            for i in range(8):
                if i < 5:
                    one(f, i, i + 2, 0)
                if i > 2:
                    one(f, i, i - 3, 1)
            return 0

        lax.fori_loop(0, 4, frame, 0)

    lax.fori_loop(0, 8, activate_frame, 0)
    reorder()
    pack(0)
    pl.semaphore_wait(barrier, greetings)
    each(own, "start")
    each(early_frames, "start", slab == 0)

    @pl.when(slab == 0)
    def _():
        to_partner.start()

    place_tile(4)
    lax.fori_loop(0, 8, mix_caches, 0)
    reorder()

    @pl.when(slab == 1)
    def _():
        pack(1)

    each(early_caches, "start", slab == 1)

    @pl.when(slab == 0)
    def _():
        place_tile(0)

    loads[7].wait()
    lay_out_weights(raw_in, wide, w_in)
    loads[8].wait()
    lay_out_weights(raw_mid, wide, w_mid)

    def clear(x, has):
        return jnp.where(has, x, 0.0)

    def unmerge(b):
        other = swap(b)
        return jnp.where(lanes16, b, other), jnp.where(lanes16, other, b)

    def place_rows(slot):
        for v, has in enumerate((up, down)):
            line, r = ((0, 0), (5, 1))[v]

            def frame(f, _):
                at = ((slot * 4 + f) * 13 + line + PAD) * LINE + r * HALF + 2
                b = unmerge(clear(got_row[slot, v, f, 2].astype(F32), has))
                for n in range(2):
                    sa[pl.ds(at + n * LINE, 16), :] = clear(got_row[slot, v, f, n].astype(F32), has)
                    sb[pl.ds(at + n * LINE, 16), :] = b[n]
                return 0

            lax.fori_loop(0, 4, frame, 0, unroll=True)

    def put_columns(s, f, j, x):
        for n in range(2):
            at = f * IMAGE + j + n
            s[pl.ds(at + (2 + PAD) * LINE, 8, stride=LINE), :] = x[8 * n : 8 * n + 8]
            s[pl.ds(at + (PAD - 3) * LINE + HALF, 8, stride=LINE), :] = x[8 * n : 8 * n + 8]

    def place_sides(slot):
        for v, has in enumerate((left, right)):
            for pair in range(2):
                b = unmerge(clear(got_side[slot, v, pair, 2].astype(F32), has))
                for e in range(2):
                    f = slot * 4 + pair * 2 + e
                    put_columns(sa, f, 18 * v, clear(got_side[slot, v, pair, e].astype(F32), has))
                    put_columns(sb, f, 18 * v, b[e])

    def place_angles(slot):
        for n, has in enumerate(there[4:]):
            for h, s in enumerate((sa, sb)):
                corner[2 * n + h] = clear(got_angle[slot, n, h].astype(F32), has)
        for n in range(4):
            line, r = ((0, 0), (5, 1))[n // 2]
            for h, s in enumerate((sa, sb)):
                for x in range(4):
                    at = slot * 4 * IMAGE + (line + x // 2 + PAD) * LINE + r * HALF + 18 * (n % 2) + x % 2
                    s[pl.ds(at, 4, stride=IMAGE), :] = corner[2 * n + h, 4 * x : 4 * x + 4, :]

    def unpack_tile():
        def frame(f, _):
            for u in range(4):
                b = unmerge(got_tile[f, u, 2].astype(F32))
                for n in range(2):
                    i = 2 * u + n
                    a = got_tile[f, u, n].astype(F32)
                    for line, r, fits in ((i + 2, 0, i < 5), (i - 3, 1, i > 2)):
                        if fits:
                            at = (f * 13 + line + PAD) * LINE + r * HALF + 2
                            sa[pl.ds(at, 16), :] = a
                            sb[pl.ds(at, 16), :] = b[n]
            return 0

        lax.fori_loop(0, 4, frame, 0)

    @pl.when(slab == 1)
    def _():
        to_partner.wait_recv()
        unpack_tile()

    each(own, "wait_recv")
    for slot in (1, 0):
        if slot == 0:
            each(early_frames, "wait_recv")
        place_rows(slot)
        place_sides(slot)
        place_angles(slot)

    def start_in(g, i, j):
        return (g * 13 + i + PAD) * LINE + j

    gather_taps(sa, sb, ta, tb, start_in, 5, 3, 5, 7, 7)
    merge_taps(tb, zp, zq, 5, 5, 7)
    result = convolve(ta, zp, zq, w_in, 3, 5, 5)
    total_a[...] = result[:, 0:128]
    total_b[...] = result[:, 128:256]

    bias_a, bias_b = halves(bias_in)
    gain_a, gain_b = halves(gain_mid)
    subs = lax.broadcasted_iota(jnp.int32, (16, 128), 0) & 7
    ones = jnp.ones((16, 128), F32)

    def activate_middle(n, _):
        i = n % 5
        gone = ((i == 0) & jnp.logical_not(up) & (subs < 4)) | ((i == 4) & jnp.logical_not(down) & (subs >= 4))
        keep_rows = jnp.where(gone, 0.0, ones)
        for j in range(5):
            start = pl.multiple_of(n * 80 + j * 16, 16)
            a = total_a[pl.ds(start, 16), :] + bias_a
            b = total_b[pl.ds(start, 16), :] + bias_b
            ya, yb = act(a, b, gain_a, gain_b, lanes16)
            keep = keep_rows
            if j == 0:
                keep = jnp.where(jnp.logical_not(left) & ((subs & 3) == 0), 0.0, keep)
            if j == 2:
                keep = jnp.where(jnp.logical_not(right) & ((subs & 3) == 3), 0.0, keep)
            mixed[pl.ds(start, 16), 0:128] = (ya * keep).astype(BF16)
            mixed[pl.ds(start, 16), 128:256] = (yb * keep).astype(BF16)
        return 0

    lax.fori_loop(0, 15, activate_middle, 0)

    def place_middle(k, _):
        start = pl.multiple_of(k * 400, 16)
        ordered = jnp.dot(mixed[pl.ds(start, 400), :], order[...], preferred_element_type=F32)
        for n in range(25):
            for h in range(2):
                at = (k + 3 * h) * MIDDLE + (n // 5) * LINE + n % 5
                y = ordered[n * 16 + 8 * h : n * 16 + 8 * h + 8]
                ma[pl.ds(at, 8, stride=5), :] = y[:, 0:128]
                mb[pl.ds(at, 8, stride=5), :] = y[:, 128:256]
        return 0

    lax.fori_loop(0, 3, place_middle, 0)

    @pl.when(slab == 0)
    def _():
        def frame(f, _):
            for n in range(10):
                line, r = (n + 1, 0) if n < 6 else (n - 4, 1)
                source = (f * 13 + line + PAD) * LINE + r * HALF + 1
                at = f * MIDDLE + (n % 5) * LINE + (n // 5) * HALF
                for s, m in ((sa, ma), (sb, mb)):
                    m[pl.ds(at, 16), :] = s[pl.ds(source, 16), :]
                    m[pl.ds(at + 16, 2), :] = s[pl.ds(source + 16, 2), :]
            return 0

        lax.fori_loop(0, 2, frame, 0)

    def start_mid(g, i, j):
        return g * MIDDLE + (i % 5) * LINE + (i // 5) * HALF + j

    gather_taps(ma, mb, ua, ub, start_mid, 2, 2, 4, 10, 4)
    merge_taps(ub, vp, vq, 4, 8, 4)
    result = convolve(ua, vp, vq, w_mid, 2, 8, 2)
    total_a[0:512] = result[:, 0:128]
    total_b[0:512] = result[:, 128:256]

    bias_a, bias_b = halves(bias_mid)

    def restore(c, _):
        for f in range(4):
            at = (f % 2) * 256 + (f // 2) * 8 + c
            ae = total_a[pl.ds(at, 8, stride=32), :] + bias_a
            be = total_b[pl.ds(at, 8, stride=32), :] + bias_b
            ao = swap(total_a[pl.ds(at + 16, 8, stride=32), :] + bias_a)
            bo = swap(total_b[pl.ds(at + 16, 8, stride=32), :] + bias_b)
            for k, branch in enumerate((ae, jnp.where(lanes8, be, ao), jnp.where(lanes8, ao, bo))):
                out[f, 3 * c + k] = (video[f, 3 * c + k].astype(F32) + branch).astype(BF16)
        return 0

    lax.fori_loop(0, 8, restore, 0)

    each(own, "wait_send")
    each(early_frames, "wait_send", slab == 0)
    each(early_caches, "wait_send", slab == 1)

    @pl.when(slab == 0)
    def _():
        to_partner.wait_send()


def body(sizes, video, cache_in, cache_mid, gain_in, gain_mid, conv_in, bias_in, conv_mid, bias_mid):
    def tiles(x):
        return x.reshape(x.shape[0], 8, 24, 128).transpose(0, 2, 1, 3)

    def taps(x):
        return x.reshape(3, 3, 864, 128).transpose(0, 2, 1, 3)

    def line(x):
        return x.reshape(1, CHAN)

    hbm, vmem = pl.BlockSpec(memory_space=pltpu.HBM), pl.BlockSpec(memory_space=pltpu.VMEM)
    scratch = [
        pltpu.VMEM((1, CHAN), F32),
        pltpu.VMEM((1, CHAN), F32),
        pltpu.VMEM((1, CHAN), F32),
        pltpu.VMEM((1, CHAN), F32),
        pltpu.VMEM((4, 24, 8, 128), BF16),
        pltpu.VMEM((2, 24, 8, 128), BF16),
        pltpu.VMEM((2, 24, 8, 128), BF16),
        pltpu.VMEM((3, 864, 3, 128), BF16),
        pltpu.VMEM((3, 864, 3, 128), BF16),
        pltpu.VMEM((3, 14 * 128, 256), BF16),
        pltpu.VMEM((3, 14 * 128, 256), BF16),
        pltpu.VMEM((4 * 24, 8, 128), F32),
        pltpu.VMEM((1200, 256), BF16),
        pltpu.VMEM((256, 256), BF16),
        pltpu.VMEM((512, 128), F32),
        pltpu.VMEM((512, 128), F32),
        pltpu.VMEM((8, 16, 128), F32),
        pltpu.VMEM((8 * IMAGE, 128), F32),
        pltpu.VMEM((8 * IMAGE, 128), F32),
        pltpu.VMEM((6 * MIDDLE, 128), F32),
        pltpu.VMEM((6 * MIDDLE, 128), F32),
        pltpu.VMEM((2, 4, 4, 3, 16, 128), BF16),
        pltpu.VMEM((2, 2, 2, 3, 16, 128), BF16),
        pltpu.VMEM((2, 4, 2, 16, 128), BF16),
        pltpu.VMEM((4, 4, 3, 16, 128), BF16),
        pltpu.VMEM((2, 2, 4, 3, 16, 128), BF16),
        pltpu.VMEM((2, 2, 2, 3, 16, 128), BF16),
        pltpu.VMEM((2, 4, 2, 16, 128), BF16),
        pltpu.VMEM((5, 7, 7, 16, 128), BF16),
        pltpu.VMEM((5, 7, 7, 16, 128), BF16),
        pltpu.VMEM((5, 5, 7, 16, 128), BF16),
        pltpu.VMEM((5, 5, 6, 16, 128), BF16),
        pltpu.VMEM((4, 10, 4, 16, 128), BF16),
        pltpu.VMEM((4, 10, 4, 16, 128), BF16),
        pltpu.VMEM((4, 8, 4, 16, 128), BF16),
        pltpu.VMEM((4, 8, 3, 16, 128), BF16),
        pltpu.VMEM((1200, 128), F32),
        pltpu.VMEM((1200, 128), F32),
        pltpu.SemaphoreType.DMA((9,)),
        pltpu.SemaphoreType.DMA((2, 8)),
        pltpu.SemaphoreType.DMA((2, 8)),
        pltpu.SemaphoreType.DMA((2,)),
    ]
    result = pl.pallas_call(
        functools.partial(kernel, sizes),
        out_shape=jax.ShapeDtypeStruct((4, 24, 8, 128), BF16),
        in_specs=[hbm] * 9,
        out_specs=vmem,
        scratch_shapes=scratch,
        compiler_params=pltpu.CompilerParams(
            collective_id=0, has_side_effects=True, vmem_limit_bytes=60 << 20),
        cost_estimate=pl.CostEstimate(flops=3_000_000_000, bytes_accessed=6_000_000, transcendentals=300_000),
    )(tiles(video), tiles(cache_in), tiles(cache_mid), line(gain_in), line(gain_mid),
      taps(conv_in), line(bias_in), taps(conv_mid), line(bias_mid))
    return result.transpose(0, 2, 1, 3).reshape(video.shape)


def solution(mesh):
    tile = P("slab", "row", "col")
    cache = P(None, "row", "col")
    sizes = (mesh.shape["row"], mesh.shape["col"])
    return jax.shard_map(
        functools.partial(body, sizes), mesh=mesh,
        in_specs=(tile, cache, cache, P(), P(), P(), P(), P(), P()),
        out_specs=tile, check_vma=False)
```

```python
import functools

import jax
import jax.numpy as jnp
from jax import lax
from jax.experimental import pallas as pl
from jax.experimental.pallas import tpu as pltpu
from jax.sharding import PartitionSpec as P

F32 = jnp.float32
BF16 = jnp.bfloat16
CHAN = 192
HALF = 20
LINE = 2 * HALF
PAD = 3
IMAGE = 13 * LINE
MIDDLE = 5 * LINE
AROUND = [(-1, 0), (1, 0), (0, -1), (0, 1), (-1, -1), (-1, 1), (1, -1), (1, 1)]


def low_lanes(shape):
    return lax.broadcasted_iota(jnp.int32, shape, len(shape) - 1) < 64


def swap(x):
    return pltpu.roll(x, 64, 1)


def act(a, b, gain_a, gain_b, lanes):
    square = a * a + jnp.where(lanes, b * b, 0.0)
    mean = jnp.sum(square, axis=1, keepdims=True) * (1.0 / CHAN)
    scale = lax.rsqrt(mean + 1e-6)
    ua, ub = a * scale * gain_a, b * scale * gain_b
    return ua / (1.0 + jnp.exp(-ua)), ub / (1.0 + jnp.exp(-ub))


def order_channels(order):
    c = lax.broadcasted_iota(jnp.int32, (256, 256), 0)
    o = lax.broadcasted_iota(jnp.int32, (256, 256), 1)
    o = jnp.where(o < CHAN, o, o - 64)
    r = o & 15
    source = (o - r) + jnp.where(r < 8, 2 * r, 2 * r - 15)
    order[...] = jnp.where(c == source, 1.0, 0.0).astype(BF16)


def lay_out_weights(raw, wide, out, a, q):
    lanes = low_lanes((8, 128))
    flat = wide.reshape(wide.shape[0] * 8, 128)
    for group in range(12):
        wide[pl.ds(group * 24, 24), 0:3, :] = raw[a, pl.ds((q * 12 + group) * 24, 24)].astype(F32)
        for p in range(3):
            first = flat[pl.ds(group * 192 + p, 8, stride=24)]
            both = flat[pl.ds(group * 192 + 8 + p, 8, stride=24)]
            second = swap(flat[pl.ds(group * 192 + 16 + p, 8, stride=24)])
            odd = jnp.where(lanes, swap(both), second)
            if group < 8:
                row = (p * 3 + q) * 128 + 16 * group
            elif p < 2:
                row = (9 + q) * 128 + 64 * p + 16 * (group - 8)
            else:
                row = 12 * 128 + 64 * (q + q // 2) + 16 * (group - 8)
            if not isinstance(row, int):
                row = pl.multiple_of(row, 16)
            out[a, pl.ds(row, 16), 0:128] = jnp.concatenate([first, odd], 0).astype(BF16)
            out[a, pl.ds(row, 16), 128:256] = jnp.concatenate([both, second], 0).astype(BF16)


def split_columns(t0, t1, t2, lanes):
    t1s, t2s = swap(t1), swap(t2)
    return [(t0, t1), (jnp.where(lanes, t1s, t2s), t2s)]


def gather_taps(sa, sb, ta, zp, zq, start_of, step, apart, pairs, rows, cols):
    size = start_of(1, 0, 0) - start_of(0, 0, 0)
    lanes = low_lanes((16, 128))

    def tile(s, at):
        first = s[pl.ds(at, 8, stride=step), :]
        second = s[pl.ds(at + apart * size, 8, stride=step), :]
        return jnp.concatenate([first, second], 0).astype(BF16)

    def body(g, _):
        last = None
        for i in range(rows):
            for j in range(cols):
                ta[g, i, j] = tile(sa, start_of(g, i, j))
            now = [tile(sb, start_of(g, i, j)) for j in range(cols)]
            if i > 0 and i < rows - 1:
                for j in range(cols):
                    zp[g, i - 1, j] = jnp.where(lanes, last[j], now[j])
            if i > 1:
                for j in range(cols - 1):
                    zq[g, i - 2, j] = jnp.where(lanes, now[j], now[j + 1])
            last = now
        return 0

    lax.fori_loop(0, pairs, body, 0)


def convolve(ta, zp, zq, weights, k, pairs, rows, cols):
    columns = []
    for a in range(3):
        g = pl.ds(k + a, pairs)
        columns += [ta[g, p : p + rows, q : q + cols] for p in range(3) for q in range(3)]
        columns += [zp[g, :, q : q + cols] for q in range(3)]
        columns += [zq[g, :, q : q + cols] for q in range(2)]
    columns = [x.reshape(pairs * rows * cols * 16, 128) for x in columns]
    weight = weights[...].reshape(3 * 14 * 128, 256)
    return jnp.dot(jnp.concatenate(columns, 1), weight, preferred_element_type=F32)


def kernel(sizes, video_hbm, cin_hbm, cmid_hbm, gin_hbm, gmid_hbm, win_hbm, bin_hbm, wmid_hbm, bmid_hbm, out,
           gain_in, gain_mid, bias_in, bias_mid, video, cin, cmid, raw_in, raw_mid, w_in, w_mid, wide, mixed, order,
           oa, ob, corner, sa, sb, ma, mb, tile, side, angle, got_tile, got_row, got_side, got_angle,
           ta, zp, zq, ua, vp, vq, total_a, total_b,
           load_sem, send_sem, recv_sem, tile_sem):
    n_row, n_col = sizes
    slab, row, col = lax.axis_index("slab"), lax.axis_index("row"), lax.axis_index("col")
    loads = [pltpu.make_async_copy(src, dst, load_sem.at[n]) for n, (src, dst) in enumerate(
        [(video_hbm, video), (cin_hbm, cin), (cmid_hbm, cmid), (gin_hbm, gain_in), (gmid_hbm, gain_mid),
         (bin_hbm, bias_in), (bmid_hbm, bias_mid), (win_hbm, raw_in), (wmid_hbm, raw_mid)])]
    for load in loads:
        load.start()

    up, down, left, right = row > 0, row < n_row - 1, col > 0, col < n_col - 1
    there = [up, down, left, right, up & left, up & right, down & left, down & right]

    def device(s, dr, dc):
        return (s, lax.rem(row + dr + n_row, n_row), lax.rem(col + dc + n_col, n_col))

    barrier = pltpu.get_barrier_semaphore()
    for s in range(2):
        for (dr, dc), has in zip(AROUND, there):
            @pl.when(has)
            def _():
                pl.semaphore_signal(barrier, inc=1, device_id=device(s, dr, dc), device_id_type=pl.DeviceIdType.MESH)
    pl.semaphore_signal(barrier, inc=1, device_id=(1 - slab, row, col), device_id_type=pl.DeviceIdType.MESH)
    n_up_down, n_sides = up.astype(jnp.int32) + down.astype(jnp.int32), left.astype(jnp.int32) + right.astype(jnp.int32)
    greetings = 2 * (n_up_down + n_sides + n_up_down * n_sides) + 1

    lanes8, lanes16 = low_lanes((8, 128)), low_lanes((16, 128))
    zero = jnp.zeros((1, 64), F32)

    def halves(ref):
        return ref[0:1, 0:128], jnp.concatenate([ref[0:1, 128:192], zero], 1)

    order_channels(order)
    for load in loads[:7]:
        load.wait()

    def columns_of(ref, f, j):
        return split_columns(*(ref[f, 3 * j + k].astype(F32) for k in range(3)), lanes8)

    def put_mixed(f, j, pixels):
        start = pl.multiple_of(f * 128 + j * 16, 16)
        mixed[pl.ds(start, 16), 0:128] = jnp.concatenate([pixels[0][0], pixels[1][0]], 0).astype(BF16)
        mixed[pl.ds(start, 16), 128:256] = jnp.concatenate([pixels[0][1], pixels[1][1]], 0).astype(BF16)

    gain_a, gain_b = halves(gain_in)

    def activate_frame(n, _):
        f = n
        for j in range(8):
            put_mixed(f, j, [act(a, b, gain_a, gain_b, lanes8) for a, b in columns_of(video, f, j)])
        return 0

    def mix_caches(j, _):
        for f in range(2):
            put_mixed(f, j, columns_of(cmid, f, j))
            put_mixed(2 + f, j, columns_of(cin, f, j))
        return 0

    def reorder():
        ordered = jnp.dot(mixed[0:512], order[...], preferred_element_type=F32)
        oa[...] = ordered[:, 0:128]
        ob[...] = ordered[:, 128:256]

    def line_of(o, f, i):
        return [o[pl.ds(f * 128 + h * 64 + i, 8, stride=8), :] for h in range(2)]

    def pack(k):
        def two_rows(n, _):
            f, u = n // 4, n % 4
            for r in range(2):
                tile[k, f, u, r] = jnp.concatenate(line_of(oa, f, 2 * u + r), 0).astype(BF16)
            b = [jnp.concatenate(line_of(ob, f, 2 * u + r), 0) for r in range(2)]
            tile[k, f, u, 2] = jnp.where(lanes16, b[0], b[1]).astype(BF16)
            return 0

        lax.fori_loop(0, 16, two_rows, 0, unroll=4)
        for v, j in enumerate((0, 14)):
            for f in range(4):
                side[k, v, f // 2, f % 2] = oa[pl.ds((f * 16 + j) * 8, 16), :].astype(BF16)
            for f in range(0, 4, 2):
                b = [ob[pl.ds(((f + e) * 16 + j) * 8, 16), :] for e in range(2)]
                side[k, v, f // 2, 2] = jnp.where(lanes16, b[0], b[1]).astype(BF16)
        for n, (i0, j0) in enumerate(((0, 0), (0, 14), (6, 0), (6, 14))):
            for h, o in enumerate((oa, ob)):
                for x in range(4):
                    at = (j0 + x % 2) * 8 + i0 + x // 2
                    corner[2 * n + h, 4 * x : 4 * x + 4, :] = o[pl.ds(at, 4, stride=128), :]
        for n in range(4):
            for h in range(2):
                angle[k, n, h] = corner[2 * n + h].astype(BF16)

    def messages(k, s, slot):
        sources = [tile.at[k, :, 0], tile.at[k, :, 3], side.at[k, 0], side.at[k, 1]] + [angle.at[k, n] for n in range(4)]
        targets = [got_row.at[slot, 1], got_row.at[slot, 0], got_side.at[slot, 1], got_side.at[slot, 0]]
        targets += [got_angle.at[slot, 3 - n] for n in range(4)]
        return [pltpu.make_async_remote_copy(
            src_ref=src, dst_ref=dst, send_sem=send_sem.at[slot, n], recv_sem=recv_sem.at[slot, n],
            device_id=device(s, dr, dc), device_id_type=pl.DeviceIdType.MESH)
            for n, (src, dst, (dr, dc)) in enumerate(zip(sources, targets, AROUND))]

    def each(copies, method, condition=None):
        exist = [there[n] for n in (1, 0, 3, 2, 7, 6, 5, 4)] if method == "wait_recv" else there
        for copy, has in zip(copies, exist):
            @pl.when(has if condition is None else has & condition)
            def _():
                getattr(copy, method)()

    own = messages(0, slab, 1)
    early_frames = messages(0, 1, 0)
    early_caches = messages(1, 0, 0)
    to_partner = pltpu.make_async_remote_copy(
        src_ref=tile.at[0], dst_ref=got_tile, send_sem=tile_sem.at[0], recv_sem=tile_sem.at[1],
        device_id=(1 - slab, row, col), device_id_type=pl.DeviceIdType.MESH)

    def place_tile(f0):
        def one(f, i, line, r):
            at = ((f0 + f) * 13 + line + PAD) * LINE + r * HALF + 2
            for o, s in ((oa, sa), (ob, sb)):
                for h, x in enumerate(line_of(o, f, i)):
                    s[pl.ds(at + 8 * h, 8), :] = x

        def frame(f, _):
            for i in range(8):
                if i < 5:
                    one(f, i, i + 2, 0)
                if i > 2:
                    one(f, i, i - 3, 1)
            return 0

        lax.fori_loop(0, 4, frame, 0)

    lax.fori_loop(0, 4, activate_frame, 0)
    reorder()
    pack(0)
    pl.semaphore_wait(barrier, greetings)
    each(own, "start")
    each(early_frames, "start", slab == 0)

    @pl.when(slab == 0)
    def _():
        to_partner.start()

    place_tile(4)
    lax.fori_loop(0, 8, mix_caches, 0, unroll=4)
    reorder()

    @pl.when(slab == 1)
    def _():
        pack(1)

    each(early_caches, "start", slab == 1)

    @pl.when(slab == 0)
    def _():
        place_tile(0)

    for w in (w_in, w_mid):
        w[:, 13 * 128 : 13 * 128 + 64, :] = jnp.zeros((3, 64, 256), BF16)
    loads[7].wait()

    def lay_out_part(n, _):
        lay_out_weights(raw_in, wide, w_in, n // 3, n % 3)
        return 0

    lax.fori_loop(0, 9, lay_out_part, 0)
    loads[8].wait()

    def clear(x, has):
        return jnp.where(has, x, 0.0)

    def unmerge(b):
        other = swap(b)
        return jnp.where(lanes16, b, other), jnp.where(lanes16, other, b)

    def place_rows(slot):
        for v, has in enumerate((up, down)):
            line, r = ((0, 0), (5, 1))[v]

            def frame(f, _):
                at = ((slot * 4 + f) * 13 + line + PAD) * LINE + r * HALF + 2
                b = unmerge(clear(got_row[slot, v, f, 2].astype(F32), has))
                for n in range(2):
                    sa[pl.ds(at + n * LINE, 16), :] = clear(got_row[slot, v, f, n].astype(F32), has)
                    sb[pl.ds(at + n * LINE, 16), :] = b[n]
                return 0

            lax.fori_loop(0, 4, frame, 0, unroll=True)

    def put_columns(s, f, j, x):
        for n in range(2):
            at = f * IMAGE + j + n
            s[pl.ds(at + (2 + PAD) * LINE, 8, stride=LINE), :] = x[8 * n : 8 * n + 8]
            s[pl.ds(at + (PAD - 3) * LINE + HALF, 8, stride=LINE), :] = x[8 * n : 8 * n + 8]

    def place_sides(slot):
        for v, has in enumerate((left, right)):
            for pair in range(2):
                b = unmerge(clear(got_side[slot, v, pair, 2].astype(F32), has))
                for e in range(2):
                    f = slot * 4 + pair * 2 + e
                    put_columns(sa, f, 18 * v, clear(got_side[slot, v, pair, e].astype(F32), has))
                    put_columns(sb, f, 18 * v, b[e])

    def place_angles(slot):
        for n, has in enumerate(there[4:]):
            for h, s in enumerate((sa, sb)):
                corner[2 * n + h] = clear(got_angle[slot, n, h].astype(F32), has)
        for n in range(4):
            line, r = ((0, 0), (5, 1))[n // 2]
            for h, s in enumerate((sa, sb)):
                for x in range(4):
                    at = slot * 4 * IMAGE + (line + x // 2 + PAD) * LINE + r * HALF + 18 * (n % 2) + x % 2
                    s[pl.ds(at, 4, stride=IMAGE), :] = corner[2 * n + h, 4 * x : 4 * x + 4, :]

    def unpack_tile():
        def frame(f, _):
            for u in range(4):
                b = unmerge(got_tile[f, u, 2].astype(F32))
                for n in range(2):
                    i = 2 * u + n
                    a = got_tile[f, u, n].astype(F32)
                    for line, r, fits in ((i + 2, 0, i < 5), (i - 3, 1, i > 2)):
                        if fits:
                            at = (f * 13 + line + PAD) * LINE + r * HALF + 2
                            sa[pl.ds(at, 16), :] = a
                            sb[pl.ds(at, 16), :] = b[n]
            return 0

        lax.fori_loop(0, 4, frame, 0)

    @pl.when(slab == 1)
    def _():
        to_partner.wait_recv()
        unpack_tile()

    each(own, "wait_recv")
    for slot in (1, 0):
        if slot == 0:
            each(early_frames, "wait_recv")
        place_rows(slot)
        place_sides(slot)
        place_angles(slot)

    def start_in(g, i, j):
        return (g * 13 + i + PAD) * LINE + j

    gather_taps(sa, sb, ta, zp, zq, start_in, 5, 3, 5, 7, 7)
    bias_a, bias_b = halves(bias_in)
    gain_a, gain_b = halves(gain_mid)
    subs = lax.broadcasted_iota(jnp.int32, (16, 128), 0) & 7

    def middle_pair(k, _):
        result = convolve(ta, zp, zq, w_in, k, 1, 5, 5)
        for q in range(3):
            lay_out_weights(raw_mid, wide, w_mid, k, q)
        total_a[0:400] = result[:, 0:128]
        total_b[0:400] = result[:, 128:256]
        for i in range(5):
            for j in range(5):
                at = (i * 5 + j) * 16
                ya, yb = act(total_a[at : at + 16, :] + bias_a, total_b[at : at + 16, :] + bias_b, gain_a, gain_b, lanes16)
                gone = []
                if i == 0:
                    gone.append(jnp.logical_not(up) & (subs < 4))
                if i == 4:
                    gone.append(jnp.logical_not(down) & (subs >= 4))
                if j == 0:
                    gone.append(jnp.logical_not(left) & ((subs & 3) == 0))
                if j == 2:
                    gone.append(jnp.logical_not(right) & ((subs & 3) == 3))
                if gone:
                    gone = functools.reduce(jnp.logical_or, gone)
                    ya, yb = jnp.where(gone, 0.0, ya), jnp.where(gone, 0.0, yb)
                mixed[at : at + 16, 0:128] = ya.astype(BF16)
                mixed[at : at + 16, 128:256] = yb.astype(BF16)
        ordered = jnp.dot(mixed[0:400], order[...], preferred_element_type=F32)
        for n in range(25):
            for h in range(2):
                at = (k + 3 * h) * MIDDLE + (n // 5) * LINE + n % 5
                y = ordered[n * 16 + 8 * h : n * 16 + 8 * h + 8]
                ma[pl.ds(at, 8, stride=5), :] = y[:, 0:128]
                mb[pl.ds(at, 8, stride=5), :] = y[:, 128:256]
        return 0

    lax.fori_loop(0, 3, middle_pair, 0)

    @pl.when(slab == 0)
    def _():
        def frame(f, _):
            for n in range(10):
                line, r = (n + 1, 0) if n < 6 else (n - 4, 1)
                source = (f * 13 + line + PAD) * LINE + r * HALF + 1
                at = f * MIDDLE + (n % 5) * LINE + (n // 5) * HALF
                for s, m in ((sa, ma), (sb, mb)):
                    m[pl.ds(at, 16), :] = s[pl.ds(source, 16), :]
                    m[pl.ds(at + 16, 2), :] = s[pl.ds(source + 16, 2), :]
            return 0

        lax.fori_loop(0, 2, frame, 0)

    def start_mid(g, i, j):
        return g * MIDDLE + (i % 5) * LINE + (i // 5) * HALF + j

    gather_taps(ma, mb, ua, vp, vq, start_mid, 2, 2, 4, 10, 4)
    result = convolve(ua, vp, vq, w_mid, 0, 2, 8, 2)
    total_a[0:512] = result[:, 0:128]
    total_b[0:512] = result[:, 128:256]

    bias_a, bias_b = halves(bias_mid)

    def restore(c, _):
        for f in range(4):
            at = (f % 2) * 256 + (f // 2) * 8 + c
            ae = total_a[pl.ds(at, 8, stride=32), :] + bias_a
            be = total_b[pl.ds(at, 8, stride=32), :] + bias_b
            ao = swap(total_a[pl.ds(at + 16, 8, stride=32), :] + bias_a)
            bo = swap(total_b[pl.ds(at + 16, 8, stride=32), :] + bias_b)
            for k, branch in enumerate((ae, jnp.where(lanes8, be, ao), jnp.where(lanes8, ao, bo))):
                out[f, 3 * c + k] = (video[f, 3 * c + k].astype(F32) + branch).astype(BF16)
        return 0

    lax.fori_loop(0, 8, restore, 0, unroll=4)

    each(own, "wait_send")
    each(early_frames, "wait_send", slab == 0)
    each(early_caches, "wait_send", slab == 1)

    @pl.when(slab == 0)
    def _():
        to_partner.wait_send()


def body(sizes, video, cache_in, cache_mid, gain_in, gain_mid, conv_in, bias_in, conv_mid, bias_mid):
    def tiles(x):
        return x.reshape(x.shape[0], 8, 24, 128).transpose(0, 2, 1, 3)

    def taps(x):
        return x.reshape(3, 3, 864, 128).transpose(0, 2, 1, 3)

    def line(x):
        return x.reshape(1, CHAN)

    hbm, vmem = pl.BlockSpec(memory_space=pltpu.HBM), pl.BlockSpec(memory_space=pltpu.VMEM)
    scratch = [
        pltpu.VMEM((1, CHAN), F32),
        pltpu.VMEM((1, CHAN), F32),
        pltpu.VMEM((1, CHAN), F32),
        pltpu.VMEM((1, CHAN), F32),
        pltpu.VMEM((4, 24, 8, 128), BF16),
        pltpu.VMEM((2, 24, 8, 128), BF16),
        pltpu.VMEM((2, 24, 8, 128), BF16),
        pltpu.VMEM((3, 864, 3, 128), BF16),
        pltpu.VMEM((3, 864, 3, 128), BF16),
        pltpu.VMEM((3, 14 * 128, 256), BF16),
        pltpu.VMEM((3, 14 * 128, 256), BF16),
        pltpu.VMEM((12 * 24, 8, 128), F32),
        pltpu.VMEM((512, 256), BF16),
        pltpu.VMEM((256, 256), BF16),
        pltpu.VMEM((512, 128), F32),
        pltpu.VMEM((512, 128), F32),
        pltpu.VMEM((8, 16, 128), F32),
        pltpu.VMEM((8 * IMAGE, 128), F32),
        pltpu.VMEM((8 * IMAGE, 128), F32),
        pltpu.VMEM((6 * MIDDLE, 128), F32),
        pltpu.VMEM((6 * MIDDLE, 128), F32),
        pltpu.VMEM((2, 4, 4, 3, 16, 128), BF16),
        pltpu.VMEM((2, 2, 2, 3, 16, 128), BF16),
        pltpu.VMEM((2, 4, 2, 16, 128), BF16),
        pltpu.VMEM((4, 4, 3, 16, 128), BF16),
        pltpu.VMEM((2, 2, 4, 3, 16, 128), BF16),
        pltpu.VMEM((2, 2, 2, 3, 16, 128), BF16),
        pltpu.VMEM((2, 4, 2, 16, 128), BF16),
        pltpu.VMEM((5, 7, 7, 16, 128), BF16),
        pltpu.VMEM((5, 5, 7, 16, 128), BF16),
        pltpu.VMEM((5, 5, 6, 16, 128), BF16),
        pltpu.VMEM((4, 10, 4, 16, 128), BF16),
        pltpu.VMEM((4, 8, 4, 16, 128), BF16),
        pltpu.VMEM((4, 8, 3, 16, 128), BF16),
        pltpu.VMEM((512, 128), F32),
        pltpu.VMEM((512, 128), F32),
        pltpu.SemaphoreType.DMA((9,)),
        pltpu.SemaphoreType.DMA((2, 8)),
        pltpu.SemaphoreType.DMA((2, 8)),
        pltpu.SemaphoreType.DMA((2,)),
    ]
    result = pl.pallas_call(
        functools.partial(kernel, sizes),
        out_shape=jax.ShapeDtypeStruct((4, 24, 8, 128), BF16),
        in_specs=[hbm] * 9,
        out_specs=vmem,
        scratch_shapes=scratch,
        compiler_params=pltpu.CompilerParams(
            collective_id=0, has_side_effects=True, vmem_limit_bytes=60 << 20),
        cost_estimate=pl.CostEstimate(flops=3_000_000_000, bytes_accessed=6_000_000, transcendentals=300_000),
    )(tiles(video), tiles(cache_in), tiles(cache_mid), line(gain_in), line(gain_mid),
      taps(conv_in), line(bias_in), taps(conv_mid), line(bias_mid))
    return result.transpose(0, 2, 1, 3).reshape(video.shape)


def solution(mesh):
    tile = P("slab", "row", "col")
    cache = P(None, "row", "col")
    sizes = (mesh.shape["row"], mesh.shape["col"])
    return jax.shard_map(
        functools.partial(body, sizes), mesh=mesh,
        in_specs=(tile, cache, cache, P(), P(), P(), P(), P(), P()),
        out_specs=tile, check_vma=False)
```

```python
import functools

import jax
import jax.numpy as jnp
from jax import lax
from jax.experimental import pallas as pl
from jax.experimental.pallas import tpu as pltpu
from jax.sharding import PartitionSpec as P

F32 = jnp.float32
BF16 = jnp.bfloat16
CHAN = 192
HALF = 20
LINE = 2 * HALF
PAD = 3
IMAGE = 13 * LINE
MIDDLE = 5 * LINE
AROUND = [(-1, 0), (1, 0), (0, -1), (0, 1), (-1, -1), (-1, 1), (1, -1), (1, 1)]
FAR_FIRST = [4, 5, 6, 7, 2, 3, 0, 1]


def low_lanes(shape):
    return lax.broadcasted_iota(jnp.int32, shape, len(shape) - 1) < 64


def swap(x):
    return pltpu.roll(x, 64, 1)


def act(a, b, gain_a, gain_b, lanes):
    square = a * a + jnp.where(lanes, b * b, 0.0)
    mean = jnp.sum(square, axis=1, keepdims=True) * (1.0 / CHAN)
    scale = lax.rsqrt(mean + 1e-6)
    ua, ub = a * scale * gain_a, b * scale * gain_b
    ua, ub = 0.5 * ua, 0.5 * ub
    return ua + ua * jnp.tanh(ua), ub + ub * jnp.tanh(ub)


def order_channels(order):
    c = lax.broadcasted_iota(jnp.int32, (256, 256), 0)
    o = lax.broadcasted_iota(jnp.int32, (256, 256), 1)
    o = jnp.where(o < CHAN, o, o - 64)
    r = o & 15
    source = (o - r) + jnp.where(r < 8, 2 * r, 2 * r - 15)
    order[...] = jnp.where(c == source, 1.0, 0.0).astype(BF16)


def lay_out_weights(raw, wide, out, a, q):
    lanes = low_lanes((8, 128))
    flat = wide.reshape(wide.shape[0] * 8, 128)
    for group in range(12):
        wide[pl.ds(group * 24, 24), 0:3, :] = raw[a, pl.ds((q * 12 + group) * 24, 24)].astype(F32)
        for p in range(3):
            first = flat[pl.ds(group * 192 + p, 8, stride=24)]
            both = flat[pl.ds(group * 192 + 8 + p, 8, stride=24)]
            second = swap(flat[pl.ds(group * 192 + 16 + p, 8, stride=24)])
            odd = jnp.where(lanes, swap(both), second)
            if group < 8:
                row = (p * 3 + q) * 128 + 16 * group
            elif p < 2:
                row = (9 + q) * 128 + 64 * p + 16 * (group - 8)
            else:
                row = 12 * 128 + 64 * (q + q // 2) + 16 * (group - 8)
            if not isinstance(row, int):
                row = pl.multiple_of(row, 16)
            out[a, pl.ds(row, 16), 0:128] = jnp.concatenate([first, odd], 0).astype(BF16)
            out[a, pl.ds(row, 16), 128:256] = jnp.concatenate([both, second], 0).astype(BF16)


def split_columns(t0, t1, t2, lanes):
    t1s, t2s = swap(t1), swap(t2)
    return [(t0, t1), (jnp.where(lanes, t1s, t2s), t2s)]


def gather_taps(sa, sb, ta, zp, zq, start_of, step, apart, pairs, rows, cols):
    size = start_of(1, 0, 0) - start_of(0, 0, 0)
    lanes = low_lanes((16, 128))

    def tile(s, at):
        first = s[pl.ds(at, 8, stride=step), :]
        second = s[pl.ds(at + apart * size, 8, stride=step), :]
        return jnp.concatenate([first, second], 0).astype(BF16)

    def body(g, _):
        last = None
        for i in range(rows):
            for j in range(cols):
                ta[g, i, j] = tile(sa, start_of(g, i, j))
            now = [tile(sb, start_of(g, i, j)) for j in range(cols)]
            if i > 0 and i < rows - 1:
                for j in range(cols):
                    zp[g, i - 1, j] = jnp.where(lanes, last[j], now[j])
            if i > 1:
                for j in range(cols - 1):
                    zq[g, i - 2, j] = jnp.where(lanes, now[j], now[j + 1])
            last = now
        return 0

    lax.fori_loop(0, pairs, body, 0)


def convolve(ta, zp, zq, weights, k, pairs, rows, cols):
    columns = []
    for a in range(3):
        g = pl.ds(k + a, pairs)
        columns += [ta[g, p : p + rows, q : q + cols] for p in range(3) for q in range(3)]
        columns += [zp[g, :, q : q + cols] for q in range(3)]
        columns += [zq[g, :, q : q + cols] for q in range(2)]
    columns = [x.reshape(pairs * rows * cols * 16, 128) for x in columns]
    weight = weights[...].reshape(3 * 14 * 128, 256)
    return jnp.dot(jnp.concatenate(columns, 1), weight, preferred_element_type=F32)


def kernel(sizes, video_hbm, cin_hbm, cmid_hbm, gin_hbm, gmid_hbm, win_hbm, bin_hbm, wmid_hbm, bmid_hbm, out,
           gain_in, gain_mid, bias_in, bias_mid, video, cin, cmid, raw_in, raw_mid, w_in, w_mid, wide, mixed, order,
           oa, ob, corner, sa, sb, ma, mb, tile, side, angle, got_tile, got_row, got_side, got_angle,
           ta, zp, zq, ua, vp, vq, total_a, total_b,
           load_sem, send_sem, recv_sem, tile_sem):
    n_row, n_col = sizes
    slab, row, col = lax.axis_index("slab"), lax.axis_index("row"), lax.axis_index("col")
    loads = [pltpu.make_async_copy(src, dst, load_sem.at[n]) for n, (src, dst) in enumerate(
        [(video_hbm, video), (cin_hbm, cin), (cmid_hbm, cmid), (gin_hbm, gain_in), (gmid_hbm, gain_mid),
         (bin_hbm, bias_in), (bmid_hbm, bias_mid), (win_hbm, raw_in), (wmid_hbm, raw_mid)])]
    for load in loads:
        load.start()

    up, down, left, right = row > 0, row < n_row - 1, col > 0, col < n_col - 1
    there = [up, down, left, right, up & left, up & right, down & left, down & right]

    def device(s, dr, dc):
        return (s, lax.rem(row + dr + n_row, n_row), lax.rem(col + dc + n_col, n_col))

    barrier = pltpu.get_barrier_semaphore()
    for s in range(2):
        for (dr, dc), has in zip(AROUND, there):
            @pl.when(has)
            def _():
                pl.semaphore_signal(barrier, inc=1, device_id=device(s, dr, dc), device_id_type=pl.DeviceIdType.MESH)
    pl.semaphore_signal(barrier, inc=1, device_id=(1 - slab, row, col), device_id_type=pl.DeviceIdType.MESH)
    n_up_down, n_sides = up.astype(jnp.int32) + down.astype(jnp.int32), left.astype(jnp.int32) + right.astype(jnp.int32)
    greetings = 2 * (n_up_down + n_sides + n_up_down * n_sides) + 1

    lanes8, lanes16 = low_lanes((8, 128)), low_lanes((16, 128))
    zero = jnp.zeros((1, 64), F32)

    def halves(ref):
        return ref[0:1, 0:128], jnp.concatenate([ref[0:1, 128:192], zero], 1)

    order_channels(order)
    for load in loads[:7]:
        load.wait()

    def columns_of(ref, f, j):
        return split_columns(*(ref[f, 3 * j + k].astype(F32) for k in range(3)), lanes8)

    def put_mixed(f, j, pixels):
        start = pl.multiple_of(f * 128 + j * 16, 16)
        mixed[0, pl.ds(start, 16), 0:128] = jnp.concatenate([pixels[0][0], pixels[1][0]], 0).astype(BF16)
        mixed[0, pl.ds(start, 16), 128:256] = jnp.concatenate([pixels[0][1], pixels[1][1]], 0).astype(BF16)

    gain_a, gain_b = halves(gain_in)

    def activate_frame(n, _):
        f = n
        for j in range(8):
            put_mixed(f, j, [act(a, b, gain_a, gain_b, lanes8) for a, b in columns_of(video, f, j)])
        return 0

    def mix_caches(j, _):
        for f in range(2):
            put_mixed(f, j, columns_of(cmid, f, j))
            put_mixed(2 + f, j, columns_of(cin, f, j))
        return 0

    def reorder():
        ordered = jnp.dot(mixed[0], order[...], preferred_element_type=F32)
        oa[...] = ordered[:, 0:128]
        ob[...] = ordered[:, 128:256]

    def line_of(o, f, i):
        return [o[pl.ds(f * 128 + h * 64 + i, 8, stride=8), :] for h in range(2)]

    def pack(k):
        def two_rows(n, _):
            f, u = n // 4, n % 4
            for r in range(2):
                tile[k, f, u, r] = jnp.concatenate(line_of(oa, f, 2 * u + r), 0).astype(BF16)
            b = [jnp.concatenate(line_of(ob, f, 2 * u + r), 0) for r in range(2)]
            tile[k, f, u, 2] = jnp.where(lanes16, b[0], b[1]).astype(BF16)
            return 0

        lax.fori_loop(0, 16, two_rows, 0, unroll=4)
        for v, j in enumerate((0, 14)):
            for f in range(4):
                side[k, v, f // 2, f % 2] = oa[pl.ds((f * 16 + j) * 8, 16), :].astype(BF16)
            for f in range(0, 4, 2):
                b = [ob[pl.ds(((f + e) * 16 + j) * 8, 16), :] for e in range(2)]
                side[k, v, f // 2, 2] = jnp.where(lanes16, b[0], b[1]).astype(BF16)
        for n, (i0, j0) in enumerate(((0, 0), (0, 14), (6, 0), (6, 14))):
            for h, o in enumerate((oa, ob)):
                for x in range(4):
                    at = (j0 + x % 2) * 8 + i0 + x // 2
                    corner[2 * n + h, 4 * x : 4 * x + 4, :] = o[pl.ds(at, 4, stride=128), :]
        for n in range(4):
            for h in range(2):
                angle[k, n, h] = corner[2 * n + h].astype(BF16)

    def messages(k, s, slot):
        sources = [tile.at[k, :, 0], tile.at[k, :, 3], side.at[k, 0], side.at[k, 1]] + [angle.at[k, n] for n in range(4)]
        targets = [got_row.at[slot, 1], got_row.at[slot, 0], got_side.at[slot, 1], got_side.at[slot, 0]]
        targets += [got_angle.at[slot, 3 - n] for n in range(4)]
        return [pltpu.make_async_remote_copy(
            src_ref=src, dst_ref=dst, send_sem=send_sem.at[slot, n], recv_sem=recv_sem.at[slot, n],
            device_id=device(s, dr, dc), device_id_type=pl.DeviceIdType.MESH)
            for n, (src, dst, (dr, dc)) in enumerate(zip(sources, targets, AROUND))]

    def each(copies, method, condition=None):
        exist = [there[n] for n in (1, 0, 3, 2, 7, 6, 5, 4)] if method == "wait_recv" else there
        for copy, has in [(copies[n], exist[n]) for n in FAR_FIRST]:
            @pl.when(has if condition is None else has & condition)
            def _():
                getattr(copy, method)()

    own = messages(0, slab, 1)
    early_frames = messages(0, 1, 0)
    early_caches = messages(1, 0, 0)
    to_partner = pltpu.make_async_remote_copy(
        src_ref=tile.at[0], dst_ref=got_tile, send_sem=tile_sem.at[0], recv_sem=tile_sem.at[1],
        device_id=(1 - slab, row, col), device_id_type=pl.DeviceIdType.MESH)

    def place_tile(f0):
        def one(f, i, line, r):
            at = ((f0 + f) * 13 + line + PAD) * LINE + r * HALF + 2
            for o, s in ((oa, sa), (ob, sb)):
                for h, x in enumerate(line_of(o, f, i)):
                    s[pl.ds(at + 8 * h, 8), :] = x

        def frame(f, _):
            for i in range(8):
                if i < 5:
                    one(f, i, i + 2, 0)
                if i > 2:
                    one(f, i, i - 3, 1)
            return 0

        lax.fori_loop(0, 4, frame, 0)

    lax.fori_loop(0, 4, activate_frame, 0)
    reorder()
    pack(0)
    pl.semaphore_wait(barrier, greetings)
    @pl.when(slab == 0)
    def _():
        to_partner.start()

    each(own, "start")
    each(early_frames, "start", slab == 0)

    place_tile(4)
    lax.fori_loop(0, 8, mix_caches, 0, unroll=4)
    reorder()

    @pl.when(slab == 1)
    def _():
        pack(1)

    each(early_caches, "start", slab == 1)

    @pl.when(slab == 0)
    def _():
        place_tile(0)

    for w in (w_in, w_mid):
        w[:, 13 * 128 : 13 * 128 + 64, :] = jnp.zeros((3, 64, 256), BF16)
    loads[7].wait()

    def lay_out_all(raw, out):
        def part(n, _):
            lay_out_weights(raw, wide, out, n // 3, n % 3)
            return 0

        lax.fori_loop(0, 9, part, 0)

    lay_out_all(raw_in, w_in)
    loads[8].wait()
    lay_out_all(raw_mid, w_mid)

    def clear(x, has):
        return jnp.where(has, x, 0.0)

    def unmerge(b):
        other = swap(b)
        return jnp.where(lanes16, b, other), jnp.where(lanes16, other, b)

    def place_rows(slot):
        for v, has in enumerate((up, down)):
            line, r = ((0, 0), (5, 1))[v]

            def frame(f, _):
                at = ((slot * 4 + f) * 13 + line + PAD) * LINE + r * HALF + 2
                b = unmerge(clear(got_row[slot, v, f, 2].astype(F32), has))
                for n in range(2):
                    sa[pl.ds(at + n * LINE, 16), :] = clear(got_row[slot, v, f, n].astype(F32), has)
                    sb[pl.ds(at + n * LINE, 16), :] = b[n]
                return 0

            lax.fori_loop(0, 4, frame, 0, unroll=True)

    def put_columns(s, f, j, x):
        for n in range(2):
            at = f * IMAGE + j + n
            s[pl.ds(at + (2 + PAD) * LINE, 8, stride=LINE), :] = x[8 * n : 8 * n + 8]
            s[pl.ds(at + (PAD - 3) * LINE + HALF, 8, stride=LINE), :] = x[8 * n : 8 * n + 8]

    def place_sides(slot):
        for v, has in enumerate((left, right)):
            for pair in range(2):
                b = unmerge(clear(got_side[slot, v, pair, 2].astype(F32), has))
                for e in range(2):
                    f = slot * 4 + pair * 2 + e
                    put_columns(sa, f, 18 * v, clear(got_side[slot, v, pair, e].astype(F32), has))
                    put_columns(sb, f, 18 * v, b[e])

    def place_angles(slot):
        for n, has in enumerate(there[4:]):
            for h, s in enumerate((sa, sb)):
                corner[2 * n + h] = clear(got_angle[slot, n, h].astype(F32), has)
        for n in range(4):
            line, r = ((0, 0), (5, 1))[n // 2]
            for h, s in enumerate((sa, sb)):
                for x in range(4):
                    at = slot * 4 * IMAGE + (line + x // 2 + PAD) * LINE + r * HALF + 18 * (n % 2) + x % 2
                    s[pl.ds(at, 4, stride=IMAGE), :] = corner[2 * n + h, 4 * x : 4 * x + 4, :]

    def unpack_tile():
        def frame(f, _):
            for u in range(4):
                b = unmerge(got_tile[f, u, 2].astype(F32))
                for n in range(2):
                    i = 2 * u + n
                    a = got_tile[f, u, n].astype(F32)
                    for line, r, fits in ((i + 2, 0, i < 5), (i - 3, 1, i > 2)):
                        if fits:
                            at = (f * 13 + line + PAD) * LINE + r * HALF + 2
                            sa[pl.ds(at, 16), :] = a
                            sb[pl.ds(at, 16), :] = b[n]
            return 0

        lax.fori_loop(0, 4, frame, 0)

    @pl.when(slab == 1)
    def _():
        to_partner.wait_recv()
        unpack_tile()

    each(own, "wait_recv")
    for slot in (1, 0):
        if slot == 0:
            each(early_frames, "wait_recv")
        place_rows(slot)
        place_sides(slot)
        place_angles(slot)

    def start_in(g, i, j):
        return (g * 13 + i + PAD) * LINE + j

    gather_taps(sa, sb, ta, zp, zq, start_in, 5, 3, 5, 7, 7)
    bias_a, bias_b = halves(bias_in)
    gain_a, gain_b = halves(gain_mid)
    subs = lax.broadcasted_iota(jnp.int32, (16, 128), 0) & 7

    def middle_pair(k, _):
        result = convolve(ta, zp, zq, w_in, k, 1, 5, 5)
        total_a[k, 0:400] = result[:, 0:128]
        total_b[k, 0:400] = result[:, 128:256]
        for i in range(5):
            for j in range(5):
                at = (i * 5 + j) * 16
                ya, yb = act(
                    total_a[k, at : at + 16, :] + bias_a, total_b[k, at : at + 16, :] + bias_b, gain_a, gain_b, lanes16)
                gone = []
                if i == 0:
                    gone.append(jnp.logical_not(up) & (subs < 4))
                if i == 4:
                    gone.append(jnp.logical_not(down) & (subs >= 4))
                if j == 0:
                    gone.append(jnp.logical_not(left) & ((subs & 3) == 0))
                if j == 2:
                    gone.append(jnp.logical_not(right) & ((subs & 3) == 3))
                if gone:
                    gone = functools.reduce(jnp.logical_or, gone)
                    ya, yb = jnp.where(gone, 0.0, ya), jnp.where(gone, 0.0, yb)
                mixed[k, at : at + 16, 0:128] = ya.astype(BF16)
                mixed[k, at : at + 16, 128:256] = yb.astype(BF16)
        ordered = jnp.dot(mixed[k, 0:400], order[...], preferred_element_type=F32)
        for n in range(25):
            for h in range(2):
                at = (k + 3 * h) * MIDDLE + (n // 5) * LINE + n % 5
                y = ordered[n * 16 + 8 * h : n * 16 + 8 * h + 8]
                ma[pl.ds(at, 8, stride=5), :] = y[:, 0:128]
                mb[pl.ds(at, 8, stride=5), :] = y[:, 128:256]
        return 0

    lax.fori_loop(0, 3, middle_pair, 0)

    @pl.when(slab == 0)
    def _():
        def frame(f, _):
            for n in range(10):
                line, r = (n + 1, 0) if n < 6 else (n - 4, 1)
                source = (f * 13 + line + PAD) * LINE + r * HALF + 1
                at = f * MIDDLE + (n % 5) * LINE + (n // 5) * HALF
                for s, m in ((sa, ma), (sb, mb)):
                    m[pl.ds(at, 16), :] = s[pl.ds(source, 16), :]
                    m[pl.ds(at + 16, 2), :] = s[pl.ds(source + 16, 2), :]
            return 0

        lax.fori_loop(0, 2, frame, 0)

    def start_mid(g, i, j):
        return g * MIDDLE + (i % 5) * LINE + (i // 5) * HALF + j

    gather_taps(ma, mb, ua, vp, vq, start_mid, 2, 2, 4, 10, 4)
    bias_a, bias_b = halves(bias_mid)

    def result_pair(k):
        result = convolve(ua, vp, vq, w_mid, k, 1, 8, 2)
        total_a[k, 0:256] = result[:, 0:128]
        total_b[k, 0:256] = result[:, 128:256]
        for h in range(2):
            f = k + 2 * h
            for c in range(8):
                at = h * 8 + c
                ae = total_a[k, pl.ds(at, 8, stride=32), :] + bias_a
                be = total_b[k, pl.ds(at, 8, stride=32), :] + bias_b
                ao = swap(total_a[k, pl.ds(at + 16, 8, stride=32), :] + bias_a)
                bo = swap(total_b[k, pl.ds(at + 16, 8, stride=32), :] + bias_b)
                for n, branch in enumerate((ae, jnp.where(lanes8, be, ao), jnp.where(lanes8, ao, bo))):
                    out[f, 3 * c + n] = (video[f, 3 * c + n].astype(F32) + branch).astype(BF16)

    for k in range(2):
        result_pair(k)

    each(own, "wait_send")
    each(early_frames, "wait_send", slab == 0)
    each(early_caches, "wait_send", slab == 1)

    @pl.when(slab == 0)
    def _():
        to_partner.wait_send()


def body(sizes, video, cache_in, cache_mid, gain_in, gain_mid, conv_in, bias_in, conv_mid, bias_mid):
    def tiles(x):
        return x.reshape(x.shape[0], 8, 24, 128).transpose(0, 2, 1, 3)

    def taps(x):
        return x.reshape(3, 3, 864, 128).transpose(0, 2, 1, 3)

    def line(x):
        return x.reshape(1, CHAN)

    hbm, vmem = pl.BlockSpec(memory_space=pltpu.HBM), pl.BlockSpec(memory_space=pltpu.VMEM)
    scratch = [
        pltpu.VMEM((1, CHAN), F32),
        pltpu.VMEM((1, CHAN), F32),
        pltpu.VMEM((1, CHAN), F32),
        pltpu.VMEM((1, CHAN), F32),
        pltpu.VMEM((4, 24, 8, 128), BF16),
        pltpu.VMEM((2, 24, 8, 128), BF16),
        pltpu.VMEM((2, 24, 8, 128), BF16),
        pltpu.VMEM((3, 864, 3, 128), BF16),
        pltpu.VMEM((3, 864, 3, 128), BF16),
        pltpu.VMEM((3, 14 * 128, 256), BF16),
        pltpu.VMEM((3, 14 * 128, 256), BF16),
        pltpu.VMEM((12 * 24, 8, 128), F32),
        pltpu.VMEM((3, 512, 256), BF16),
        pltpu.VMEM((256, 256), BF16),
        pltpu.VMEM((512, 128), F32),
        pltpu.VMEM((512, 128), F32),
        pltpu.VMEM((8, 16, 128), F32),
        pltpu.VMEM((8 * IMAGE, 128), F32),
        pltpu.VMEM((8 * IMAGE, 128), F32),
        pltpu.VMEM((6 * MIDDLE, 128), F32),
        pltpu.VMEM((6 * MIDDLE, 128), F32),
        pltpu.VMEM((2, 4, 4, 3, 16, 128), BF16),
        pltpu.VMEM((2, 2, 2, 3, 16, 128), BF16),
        pltpu.VMEM((2, 4, 2, 16, 128), BF16),
        pltpu.VMEM((4, 4, 3, 16, 128), BF16),
        pltpu.VMEM((2, 2, 4, 3, 16, 128), BF16),
        pltpu.VMEM((2, 2, 2, 3, 16, 128), BF16),
        pltpu.VMEM((2, 4, 2, 16, 128), BF16),
        pltpu.VMEM((5, 7, 7, 16, 128), BF16),
        pltpu.VMEM((5, 5, 7, 16, 128), BF16),
        pltpu.VMEM((5, 5, 6, 16, 128), BF16),
        pltpu.VMEM((4, 10, 4, 16, 128), BF16),
        pltpu.VMEM((4, 8, 4, 16, 128), BF16),
        pltpu.VMEM((4, 8, 3, 16, 128), BF16),
        pltpu.VMEM((3, 400, 128), F32),
        pltpu.VMEM((3, 400, 128), F32),
        pltpu.SemaphoreType.DMA((9,)),
        pltpu.SemaphoreType.DMA((2, 8)),
        pltpu.SemaphoreType.DMA((2, 8)),
        pltpu.SemaphoreType.DMA((2,)),
    ]
    result = pl.pallas_call(
        functools.partial(kernel, sizes),
        out_shape=jax.ShapeDtypeStruct((4, 24, 8, 128), BF16),
        in_specs=[hbm] * 9,
        out_specs=vmem,
        scratch_shapes=scratch,
        compiler_params=pltpu.CompilerParams(
            collective_id=0, has_side_effects=True, vmem_limit_bytes=52 << 20),
        cost_estimate=pl.CostEstimate(flops=3_000_000_000, bytes_accessed=6_000_000, transcendentals=300_000),
    )(*(pltpu.with_memory_space_constraint(x, pltpu.HBM) for x in (
        tiles(video), tiles(cache_in), tiles(cache_mid), line(gain_in), line(gain_mid),
        taps(conv_in), line(bias_in), taps(conv_mid), line(bias_mid))))
    return result.transpose(0, 2, 1, 3).reshape(video.shape)


def solution(mesh):
    tile = P("slab", "row", "col")
    cache = P(None, "row", "col")
    sizes = (mesh.shape["row"], mesh.shape["col"])
    return jax.shard_map(
        functools.partial(body, sizes), mesh=mesh,
        in_specs=(tile, cache, cache, P(), P(), P(), P(), P(), P()),
        out_specs=tile, check_vma=False)
```

```python
import functools

import jax
import jax.numpy as jnp
from jax import lax
from jax.experimental import pallas as pl
from jax.experimental.pallas import tpu as pltpu
from jax.sharding import PartitionSpec as P

F32 = jnp.float32
BF16 = jnp.bfloat16
CHAN = 192
HALF = 20
LINE = 2 * HALF
PAD = 3
IMAGE = 13 * LINE
MIDDLE = 5 * LINE
AROUND = [(-1, 0), (1, 0), (0, -1), (0, 1), (-1, -1), (-1, 1), (1, -1), (1, 1)]
FAR_FIRST = [4, 5, 6, 7, 2, 3, 0, 1]


def low_lanes(shape):
    return lax.broadcasted_iota(jnp.int32, shape, len(shape) - 1) < 64


def swap(x):
    return pltpu.roll(x, 64, 1)


def act(a, b, gain_a, gain_b, lanes):
    square = a * a + jnp.where(lanes, b * b, 0.0)
    mean = jnp.sum(square, axis=1, keepdims=True) * (1.0 / CHAN)
    scale = lax.rsqrt(mean + 1e-6)
    ua, ub = a * scale * gain_a, b * scale * gain_b
    ua, ub = 0.5 * ua, 0.5 * ub
    return ua + ua * jnp.tanh(ua), ub + ub * jnp.tanh(ub)


def order_channels(order):
    c = lax.broadcasted_iota(jnp.int32, (256, 256), 0)
    o = lax.broadcasted_iota(jnp.int32, (256, 256), 1)
    o = jnp.where(o < CHAN, o, o - 64)
    r = o & 15
    source = (o - r) + jnp.where(r < 8, 2 * r, 2 * r - 15)
    order[...] = jnp.where(c == source, 1.0, 0.0).astype(BF16)


def lay_out_weights(raw, wide, out, a, q):
    lanes = low_lanes((8, 128))
    flat = wide.reshape(wide.shape[0] * 8, 128)
    for group in range(12):
        wide[pl.ds(group * 24, 24), 0:3, :] = raw[a, pl.ds((q * 12 + group) * 24, 24)].astype(F32)
        for p in range(3):
            first = flat[pl.ds(group * 192 + p, 8, stride=24)]
            both = flat[pl.ds(group * 192 + 8 + p, 8, stride=24)]
            second = swap(flat[pl.ds(group * 192 + 16 + p, 8, stride=24)])
            odd = jnp.where(lanes, swap(both), second)
            if group < 8:
                row = (p * 3 + q) * 128 + 16 * group
            elif p < 2:
                row = (9 + q) * 128 + 64 * p + 16 * (group - 8)
            else:
                row = 12 * 128 + 64 * (q + q // 2) + 16 * (group - 8)
            if not isinstance(row, int):
                row = pl.multiple_of(row, 16)
            out[a, pl.ds(row, 16), 0:128] = jnp.concatenate([first, odd], 0).astype(BF16)
            out[a, pl.ds(row, 16), 128:256] = jnp.concatenate([both, second], 0).astype(BF16)


def split_columns(t0, t1, t2, lanes):
    t1s, t2s = swap(t1), swap(t2)
    return [(t0, t1), (jnp.where(lanes, t1s, t2s), t2s)]


def gather_taps(sa, sb, ta, zp, zq, start_of, step, apart, first_pair, pairs, rows, cols):
    size = start_of(1, 0, 0) - start_of(0, 0, 0)
    lanes = low_lanes((16, 128))

    def tile(s, at):
        first = s[pl.ds(at, 8, stride=step), :]
        second = s[pl.ds(at + apart * size, 8, stride=step), :]
        return jnp.concatenate([first, second], 0).astype(BF16)

    def body(g, _):
        last = None
        for i in range(rows):
            for j in range(cols):
                ta[g, i, j] = tile(sa, start_of(g, i, j))
            now = [tile(sb, start_of(g, i, j)) for j in range(cols)]
            if i > 0 and i < rows - 1:
                for j in range(cols):
                    zp[g, i - 1, j] = jnp.where(lanes, last[j], now[j])
            if i > 1:
                for j in range(cols - 1):
                    zq[g, i - 2, j] = jnp.where(lanes, now[j], now[j + 1])
            last = now
        return 0

    lax.fori_loop(first_pair, pairs, body, 0)


def convolve(ta, zp, zq, weights, k, pairs, rows, cols):
    columns = []
    for a in range(3):
        g = pl.ds(k + a, pairs)
        columns += [ta[g, p : p + rows, q : q + cols] for p in range(3) for q in range(3)]
        columns += [zp[g, :, q : q + cols] for q in range(3)]
        columns += [zq[g, :, q : q + cols] for q in range(2)]
    columns = [x.reshape(pairs * rows * cols * 16, 128) for x in columns]
    weight = weights[...].reshape(3 * 14 * 128, 256)
    return jnp.dot(jnp.concatenate(columns, 1), weight, preferred_element_type=F32)


def kernel(sizes, video_hbm, cin_hbm, cmid_hbm, gin_hbm, gmid_hbm, win_hbm, bin_hbm, wmid_hbm, bmid_hbm, out,
           gain_in, gain_mid, bias_in, bias_mid, video, cin, cmid, raw_in, raw_mid, w_in, w_mid, wide, mixed, order,
           oa, ob, corner, sa, sb, ma, mb, tile, side, angle, got_tile, got_row, got_side, got_angle,
           ta, zp, zq, ua, vp, vq, total_a, total_b,
           load_sem, send_sem, recv_sem, tile_sem):
    n_row, n_col = sizes
    slab, row, col = lax.axis_index("slab"), lax.axis_index("row"), lax.axis_index("col")
    loads = [pltpu.make_async_copy(src, dst, load_sem.at[n]) for n, (src, dst) in enumerate(
        [(video_hbm, video), (cin_hbm, cin), (cmid_hbm, cmid), (gin_hbm, gain_in), (gmid_hbm, gain_mid),
         (bin_hbm, bias_in), (bmid_hbm, bias_mid), (win_hbm, raw_in), (wmid_hbm, raw_mid)])]

    up, down, left, right = row > 0, row < n_row - 1, col > 0, col < n_col - 1
    there = [up, down, left, right, up & left, up & right, down & left, down & right]

    def device(s, dr, dc):
        return (s, lax.rem(row + dr + n_row, n_row), lax.rem(col + dc + n_col, n_col))

    barrier = pltpu.get_barrier_semaphore()
    for s in range(2):
        for (dr, dc), has in zip(AROUND, there):
            @pl.when(has)
            def _():
                pl.semaphore_signal(barrier, inc=1, device_id=device(s, dr, dc), device_id_type=pl.DeviceIdType.MESH)
    pl.semaphore_signal(barrier, inc=1, device_id=(1 - slab, row, col), device_id_type=pl.DeviceIdType.MESH)
    n_up_down, n_sides = up.astype(jnp.int32) + down.astype(jnp.int32), left.astype(jnp.int32) + right.astype(jnp.int32)
    greetings = 2 * (n_up_down + n_sides + n_up_down * n_sides) + 1

    lanes8, lanes16 = low_lanes((8, 128)), low_lanes((16, 128))
    zero = jnp.zeros((1, 64), F32)

    def halves(ref):
        return ref[0:1, 0:128], jnp.concatenate([ref[0:1, 128:192], zero], 1)

    for load in loads:
        load.start()

    order_channels(order)
    for load in loads[:7]:
        load.wait()

    def columns_of(ref, f, j):
        return split_columns(*(ref[f, 3 * j + k].astype(F32) for k in range(3)), lanes8)

    def put_mixed(f, j, pixels):
        start = pl.multiple_of(f * 128 + j * 16, 16)
        mixed[0, pl.ds(start, 16), 0:128] = jnp.concatenate([pixels[0][0], pixels[1][0]], 0).astype(BF16)
        mixed[0, pl.ds(start, 16), 128:256] = jnp.concatenate([pixels[0][1], pixels[1][1]], 0).astype(BF16)

    gain_a, gain_b = halves(gain_in)

    def activate_frame(n, _):
        f = n
        for j in range(8):
            put_mixed(f, j, [act(a, b, gain_a, gain_b, lanes8) for a, b in columns_of(video, f, j)])
        return 0

    def mix_caches(j, _):
        for f in range(2):
            put_mixed(f, j, columns_of(cmid, f, j))
            put_mixed(2 + f, j, columns_of(cin, f, j))
        return 0

    def reorder():
        ordered = jnp.dot(mixed[0], order[...], preferred_element_type=F32)
        oa[...] = ordered[:, 0:128]
        ob[...] = ordered[:, 128:256]

    def line_of(o, f, i):
        return [o[pl.ds(f * 128 + h * 64 + i, 8, stride=8), :] for h in range(2)]

    def pack(k):
        def two_rows(n, _):
            f, u = n // 4, n % 4
            for r in range(2):
                tile[k, f, u, r] = jnp.concatenate(line_of(oa, f, 2 * u + r), 0).astype(BF16)
            b = [jnp.concatenate(line_of(ob, f, 2 * u + r), 0) for r in range(2)]
            tile[k, f, u, 2] = jnp.where(lanes16, b[0], b[1]).astype(BF16)
            return 0

        lax.fori_loop(0, 16, two_rows, 0, unroll=4)
        for v, j in enumerate((0, 14)):
            for f in range(4):
                side[k, v, f // 2, f % 2] = oa[pl.ds((f * 16 + j) * 8, 16), :].astype(BF16)
            for f in range(0, 4, 2):
                b = [ob[pl.ds(((f + e) * 16 + j) * 8, 16), :] for e in range(2)]
                side[k, v, f // 2, 2] = jnp.where(lanes16, b[0], b[1]).astype(BF16)
        for n, (i0, j0) in enumerate(((0, 0), (0, 14), (6, 0), (6, 14))):
            for h, o in enumerate((oa, ob)):
                for x in range(4):
                    at = (j0 + x % 2) * 8 + i0 + x // 2
                    corner[2 * n + h, 4 * x : 4 * x + 4, :] = o[pl.ds(at, 4, stride=128), :]
        for n in range(4):
            for h in range(2):
                angle[k, n, h] = corner[2 * n + h].astype(BF16)

    def messages(k, s, slot):
        sources = [tile.at[k, :, 0], tile.at[k, :, 3], side.at[k, 0], side.at[k, 1]] + [angle.at[k, n] for n in range(4)]
        targets = [got_row.at[slot, 1], got_row.at[slot, 0], got_side.at[slot, 1], got_side.at[slot, 0]]
        targets += [got_angle.at[slot, 3 - n] for n in range(4)]
        return [pltpu.make_async_remote_copy(
            src_ref=src, dst_ref=dst, send_sem=send_sem.at[slot, n], recv_sem=recv_sem.at[slot, n],
            device_id=device(s, dr, dc), device_id_type=pl.DeviceIdType.MESH)
            for n, (src, dst, (dr, dc)) in enumerate(zip(sources, targets, AROUND))]

    def each(copies, method, condition=None):
        exist = [there[n] for n in (1, 0, 3, 2, 7, 6, 5, 4)] if method == "wait_recv" else there
        for copy, has in [(copies[n], exist[n]) for n in FAR_FIRST]:
            @pl.when(has if condition is None else has & condition)
            def _():
                getattr(copy, method)()

    own = messages(0, slab, 1)
    early_frames = messages(0, 1, 0)
    early_caches = messages(1, 0, 0)
    to_partner = pltpu.make_async_remote_copy(
        src_ref=tile.at[0], dst_ref=got_tile, send_sem=tile_sem.at[0], recv_sem=tile_sem.at[1],
        device_id=(1 - slab, row, col), device_id_type=pl.DeviceIdType.MESH)

    def place_tile(f0):
        def one(f, i, line, r):
            at = ((f0 + f) * 13 + line + PAD) * LINE + r * HALF + 2
            for o, s in ((oa, sa), (ob, sb)):
                for h, x in enumerate(line_of(o, f, i)):
                    s[pl.ds(at + 8 * h, 8), :] = x

        def frame(f, _):
            for i in range(8):
                if i < 5:
                    one(f, i, i + 2, 0)
                if i > 2:
                    one(f, i, i - 3, 1)
            return 0

        lax.fori_loop(0, 4, frame, 0)

    lax.fori_loop(0, 4, activate_frame, 0)
    reorder()
    pack(0)
    pl.semaphore_wait(barrier, greetings)
    @pl.when(slab == 0)
    def _():
        to_partner.start()

    each(early_frames, "start", slab == 0)
    each(own, "start")

    place_tile(4)
    lax.fori_loop(0, 8, mix_caches, 0, unroll=4)
    reorder()

    @pl.when(slab == 1)
    def _():
        pack(1)

    each(early_caches, "start", slab == 1)

    @pl.when(slab == 0)
    def _():
        place_tile(0)

    for w in (w_in, w_mid):
        w[:, 13 * 128 : 13 * 128 + 64, :] = jnp.zeros((3, 64, 256), BF16)
    loads[7].wait()

    def lay_out_all(raw, out):
        def part(n, _):
            lay_out_weights(raw, wide, out, n // 3, n % 3)
            return 0

        lax.fori_loop(0, 9, part, 0)

    lay_out_all(raw_in, w_in)
    loads[8].wait()
    lay_out_all(raw_mid, w_mid)

    def clear(x, has):
        return jnp.where(has, x, 0.0)

    def unmerge(b):
        other = swap(b)
        return jnp.where(lanes16, b, other), jnp.where(lanes16, other, b)

    def place_rows(slot):
        for v, has in enumerate((up, down)):
            line, r = ((0, 0), (5, 1))[v]

            def frame(f, _):
                at = ((slot * 4 + f) * 13 + line + PAD) * LINE + r * HALF + 2
                b = unmerge(clear(got_row[slot, v, f, 2].astype(F32), has))
                for n in range(2):
                    sa[pl.ds(at + n * LINE, 16), :] = clear(got_row[slot, v, f, n].astype(F32), has)
                    sb[pl.ds(at + n * LINE, 16), :] = b[n]
                return 0

            lax.fori_loop(0, 4, frame, 0, unroll=True)

    def put_columns(s, f, j, x):
        for n in range(2):
            at = f * IMAGE + j + n
            s[pl.ds(at + (2 + PAD) * LINE, 8, stride=LINE), :] = x[8 * n : 8 * n + 8]
            s[pl.ds(at + (PAD - 3) * LINE + HALF, 8, stride=LINE), :] = x[8 * n : 8 * n + 8]

    def place_sides(slot):
        for v, has in enumerate((left, right)):
            for pair in range(2):
                b = unmerge(clear(got_side[slot, v, pair, 2].astype(F32), has))
                for e in range(2):
                    f = slot * 4 + pair * 2 + e
                    put_columns(sa, f, 18 * v, clear(got_side[slot, v, pair, e].astype(F32), has))
                    put_columns(sb, f, 18 * v, b[e])

    def place_angles(slot):
        for n, has in enumerate(there[4:]):
            for h, s in enumerate((sa, sb)):
                corner[2 * n + h] = clear(got_angle[slot, n, h].astype(F32), has)
        for n in range(4):
            line, r = ((0, 0), (5, 1))[n // 2]
            for h, s in enumerate((sa, sb)):
                for x in range(4):
                    at = slot * 4 * IMAGE + (line + x // 2 + PAD) * LINE + r * HALF + 18 * (n % 2) + x % 2
                    s[pl.ds(at, 4, stride=IMAGE), :] = corner[2 * n + h, 4 * x : 4 * x + 4, :]

    def unpack_tile():
        def frame(f, _):
            for u in range(4):
                b = unmerge(got_tile[f, u, 2].astype(F32))
                for n in range(2):
                    i = 2 * u + n
                    a = got_tile[f, u, n].astype(F32)
                    for line, r, fits in ((i + 2, 0, i < 5), (i - 3, 1, i > 2)):
                        if fits:
                            at = (f * 13 + line + PAD) * LINE + r * HALF + 2
                            sa[pl.ds(at, 16), :] = a
                            sb[pl.ds(at, 16), :] = b[n]
            return 0

        lax.fori_loop(0, 4, frame, 0)

    @pl.when(slab == 1)
    def _():
        to_partner.wait_recv()
        unpack_tile()

    each(own, "wait_recv")
    for slot in (1, 0):
        if slot == 0:
            each(early_frames, "wait_recv")
        place_rows(slot)
        place_sides(slot)
        place_angles(slot)

    def start_in(g, i, j):
        return (g * 13 + i + PAD) * LINE + j

    gather_taps(sa, sb, ta, zp, zq, start_in, 5, 1, 2 - 2 * slab, 7, 7, 7)
    bias_a, bias_b = halves(bias_in)
    gain_a, gain_b = halves(gain_mid)
    subs = lax.broadcasted_iota(jnp.int32, (16, 128), 0) & 7

    def middle_pair(k, _):
        result = convolve(ta, zp, zq, w_in, 2 * k, 1, 5, 5)
        total_a[k, 0:400] = result[:, 0:128]
        total_b[k, 0:400] = result[:, 128:256]
        for i in range(5):
            for j in range(5):
                at = (i * 5 + j) * 16
                ya, yb = act(
                    total_a[k, at : at + 16, :] + bias_a, total_b[k, at : at + 16, :] + bias_b, gain_a, gain_b, lanes16)
                gone = []
                if i == 0:
                    gone.append(jnp.logical_not(up) & (subs < 4))
                if i == 4:
                    gone.append(jnp.logical_not(down) & (subs >= 4))
                if j == 0:
                    gone.append(jnp.logical_not(left) & ((subs & 3) == 0))
                if j == 2:
                    gone.append(jnp.logical_not(right) & ((subs & 3) == 3))
                if gone:
                    gone = functools.reduce(jnp.logical_or, gone)
                    ya, yb = jnp.where(gone, 0.0, ya), jnp.where(gone, 0.0, yb)
                mixed[k, at : at + 16, 0:128] = ya.astype(BF16)
                mixed[k, at : at + 16, 128:256] = yb.astype(BF16)
        ordered = jnp.dot(mixed[k, 0:400], order[...], preferred_element_type=F32)
        for n in range(25):
            for h in range(2):
                at = (2 * k + h) * MIDDLE + (n // 5) * LINE + n % 5
                y = ordered[n * 16 + 8 * h : n * 16 + 8 * h + 8]
                ma[pl.ds(at, 8, stride=5), :] = y[:, 0:128]
                mb[pl.ds(at, 8, stride=5), :] = y[:, 128:256]
        return 0

    lax.fori_loop(1 - slab, 3, middle_pair, 0)

    @pl.when(slab == 0)
    def _():
        def frame(f, _):
            for n in range(10):
                line, r = (n + 1, 0) if n < 6 else (n - 4, 1)
                source = (f * 13 + line + PAD) * LINE + r * HALF + 1
                at = f * MIDDLE + (n % 5) * LINE + (n // 5) * HALF
                for s, m in ((sa, ma), (sb, mb)):
                    m[pl.ds(at, 16), :] = s[pl.ds(source, 16), :]
                    m[pl.ds(at + 16, 2), :] = s[pl.ds(source + 16, 2), :]
            return 0

        lax.fori_loop(0, 2, frame, 0)

    def start_mid(g, i, j):
        return g * MIDDLE + (i % 5) * LINE + (i // 5) * HALF + j

    gather_taps(ma, mb, ua, vp, vq, start_mid, 2, 2, 0, 4, 10, 4)
    bias_a, bias_b = halves(bias_mid)

    def result_pair(k):
        result = convolve(ua, vp, vq, w_mid, k, 1, 8, 2)
        total_a[k, 0:256] = result[:, 0:128]
        total_b[k, 0:256] = result[:, 128:256]
        for h in range(2):
            f = k + 2 * h
            for c in range(8):
                at = h * 8 + c
                ae = total_a[k, pl.ds(at, 8, stride=32), :] + bias_a
                be = total_b[k, pl.ds(at, 8, stride=32), :] + bias_b
                ao = swap(total_a[k, pl.ds(at + 16, 8, stride=32), :] + bias_a)
                bo = swap(total_b[k, pl.ds(at + 16, 8, stride=32), :] + bias_b)
                for n, branch in enumerate((ae, jnp.where(lanes8, be, ao), jnp.where(lanes8, ao, bo))):
                    out[f, 3 * c + n] = (video[f, 3 * c + n].astype(F32) + branch).astype(BF16)

    for k in range(2):
        result_pair(k)

    each(own, "wait_send")
    each(early_frames, "wait_send", slab == 0)
    each(early_caches, "wait_send", slab == 1)

    @pl.when(slab == 0)
    def _():
        to_partner.wait_send()


def body(sizes, video, cache_in, cache_mid, gain_in, gain_mid, conv_in, bias_in, conv_mid, bias_mid):
    def tiles(x):
        return x.reshape(x.shape[0], 8, 24, 128).transpose(0, 2, 1, 3)

    def taps(x):
        return x.reshape(3, 3, 864, 128).transpose(0, 2, 1, 3)

    def line(x):
        return x.reshape(1, CHAN)

    hbm, vmem = pl.BlockSpec(memory_space=pltpu.HBM), pl.BlockSpec(memory_space=pltpu.VMEM)
    scratch = [
        pltpu.VMEM((1, CHAN), F32),
        pltpu.VMEM((1, CHAN), F32),
        pltpu.VMEM((1, CHAN), F32),
        pltpu.VMEM((1, CHAN), F32),
        pltpu.VMEM((4, 24, 8, 128), BF16),
        pltpu.VMEM((2, 24, 8, 128), BF16),
        pltpu.VMEM((2, 24, 8, 128), BF16),
        pltpu.VMEM((3, 864, 3, 128), BF16),
        pltpu.VMEM((3, 864, 3, 128), BF16),
        pltpu.VMEM((3, 14 * 128, 256), BF16),
        pltpu.VMEM((3, 14 * 128, 256), BF16),
        pltpu.VMEM((12 * 24, 8, 128), F32),
        pltpu.VMEM((3, 512, 256), BF16),
        pltpu.VMEM((256, 256), BF16),
        pltpu.VMEM((512, 128), F32),
        pltpu.VMEM((512, 128), F32),
        pltpu.VMEM((8, 16, 128), F32),
        pltpu.VMEM((8 * IMAGE, 128), F32),
        pltpu.VMEM((8 * IMAGE, 128), F32),
        pltpu.VMEM((6 * MIDDLE, 128), F32),
        pltpu.VMEM((6 * MIDDLE, 128), F32),
        pltpu.VMEM((2, 4, 4, 3, 16, 128), BF16),
        pltpu.VMEM((2, 2, 2, 3, 16, 128), BF16),
        pltpu.VMEM((2, 4, 2, 16, 128), BF16),
        pltpu.VMEM((4, 4, 3, 16, 128), BF16),
        pltpu.VMEM((2, 2, 4, 3, 16, 128), BF16),
        pltpu.VMEM((2, 2, 2, 3, 16, 128), BF16),
        pltpu.VMEM((2, 4, 2, 16, 128), BF16),
        pltpu.VMEM((7, 7, 7, 16, 128), BF16),
        pltpu.VMEM((7, 5, 7, 16, 128), BF16),
        pltpu.VMEM((7, 5, 6, 16, 128), BF16),
        pltpu.VMEM((4, 10, 4, 16, 128), BF16),
        pltpu.VMEM((4, 8, 4, 16, 128), BF16),
        pltpu.VMEM((4, 8, 3, 16, 128), BF16),
        pltpu.VMEM((3, 400, 128), F32),
        pltpu.VMEM((3, 400, 128), F32),
        pltpu.SemaphoreType.DMA((9,)),
        pltpu.SemaphoreType.DMA((2, 8)),
        pltpu.SemaphoreType.DMA((2, 8)),
        pltpu.SemaphoreType.DMA((2,)),
    ]
    result = pl.pallas_call(
        functools.partial(kernel, sizes),
        out_shape=jax.ShapeDtypeStruct((4, 24, 8, 128), BF16),
        in_specs=[hbm] * 9,
        out_specs=vmem,
        scratch_shapes=scratch,
        compiler_params=pltpu.CompilerParams(
            collective_id=0, has_side_effects=True, vmem_limit_bytes=52 << 20),
        cost_estimate=pl.CostEstimate(flops=3_000_000_000, bytes_accessed=6_000_000, transcendentals=300_000),
    )(*(pltpu.with_memory_space_constraint(x, pltpu.HBM) for x in (
        tiles(video), tiles(cache_in), tiles(cache_mid), line(gain_in), line(gain_mid),
        taps(conv_in), line(bias_in), taps(conv_mid), line(bias_mid))))
    return result.transpose(0, 2, 1, 3).reshape(video.shape)


def solution(mesh):
    tile = P("slab", "row", "col")
    cache = P(None, "row", "col")
    sizes = (mesh.shape["row"], mesh.shape["col"])
    return jax.shard_map(
        functools.partial(body, sizes), mesh=mesh,
        in_specs=(tile, cache, cache, P(), P(), P(), P(), P(), P()),
        out_specs=tile, check_vma=False)
```

```python
import functools

import jax
import jax.numpy as jnp
from jax import lax
from jax.experimental import pallas as pl
from jax.experimental.pallas import tpu as pltpu
from jax.sharding import PartitionSpec as P

F32 = jnp.float32
BF16 = jnp.bfloat16
CHAN = 192
HALF = 20
LINE = 2 * HALF
PAD = 3
IMAGE = 13 * LINE
MIDDLE = 5 * LINE
AROUND = [(-1, 0), (1, 0), (0, -1), (0, 1), (-1, -1), (-1, 1), (1, -1), (1, 1)]
FAR_FIRST = [4, 5, 6, 7, 2, 3, 0, 1]


def low_lanes(shape):
    return lax.broadcasted_iota(jnp.int32, shape, len(shape) - 1) < 64


def swap(x):
    return pltpu.roll(x, 64, 1)


def act(a, b, gain_a, gain_b, lanes):
    square = a * a + jnp.where(lanes, b * b, 0.0)
    mean = jnp.sum(square, axis=1, keepdims=True) * (1.0 / CHAN)
    scale = lax.rsqrt(mean + 1e-6)
    ua, ub = a * scale * gain_a, b * scale * gain_b
    ua, ub = 0.5 * ua, 0.5 * ub
    return ua + ua * jnp.tanh(ua), ub + ub * jnp.tanh(ub)


def order_channels(order):
    c = lax.broadcasted_iota(jnp.int32, (256, 256), 0)
    o = lax.broadcasted_iota(jnp.int32, (256, 256), 1)
    o = jnp.where(o < CHAN, o, o - 64)
    r = o & 15
    source = (o - r) + jnp.where(r < 8, 2 * r, 2 * r - 15)
    order[...] = jnp.where(c == source, 1.0, 0.0).astype(BF16)


def lay_out_weights(raw, wide, out, a, q):
    lanes = low_lanes((8, 128))
    flat = wide.reshape(wide.shape[0] * 8, 128)
    for group in range(12):
        wide[pl.ds(group * 24, 24), 0:3, :] = raw[a, pl.ds((q * 12 + group) * 24, 24)].astype(F32)
        for p in range(3):
            first = flat[pl.ds(group * 192 + p, 8, stride=24)]
            both = flat[pl.ds(group * 192 + 8 + p, 8, stride=24)]
            second = swap(flat[pl.ds(group * 192 + 16 + p, 8, stride=24)])
            odd = jnp.where(lanes, swap(both), second)
            if group < 8:
                row = (p * 3 + q) * 128 + 16 * group
            elif p < 2:
                row = (9 + q) * 128 + 64 * p + 16 * (group - 8)
            else:
                row = 12 * 128 + 64 * (q + q // 2) + 16 * (group - 8)
            if not isinstance(row, int):
                row = pl.multiple_of(row, 16)
            out[a, pl.ds(row, 16), 0:128] = jnp.concatenate([first, odd], 0).astype(BF16)
            out[a, pl.ds(row, 16), 128:256] = jnp.concatenate([both, second], 0).astype(BF16)


def split_columns(t0, t1, t2, lanes):
    t1s, t2s = swap(t1), swap(t2)
    return [(t0, t1), (jnp.where(lanes, t1s, t2s), t2s)]


def gather_taps(sa, sb, ta, zp, zq, start_of, step, apart, first_pair, pairs, rows, cols):
    size = start_of(1, 0, 0) - start_of(0, 0, 0)
    lanes = low_lanes((16, 128))

    def tile(s, at):
        first = s[pl.ds(at, 8, stride=step), :]
        second = s[pl.ds(at + apart * size, 8, stride=step), :]
        return jnp.concatenate([first, second], 0).astype(BF16)

    def body(g, _):
        last = None
        for i in range(rows):
            for j in range(cols):
                ta[g, i, j] = tile(sa, start_of(g, i, j))
            now = [tile(sb, start_of(g, i, j)) for j in range(cols)]
            if i > 0 and i < rows - 1:
                for j in range(cols):
                    zp[g, i - 1, j] = jnp.where(lanes, last[j], now[j])
            if i > 1:
                for j in range(cols - 1):
                    zq[g, i - 2, j] = jnp.where(lanes, now[j], now[j + 1])
            last = now
        return 0

    lax.fori_loop(first_pair, pairs, body, 0)


def convolve(ta, zp, zq, weights, k, pairs, rows, cols):
    columns = []
    for a in range(3):
        g = pl.ds(k + a, pairs)
        columns += [ta[g, p : p + rows, q : q + cols] for p in range(3) for q in range(3)]
        columns += [zp[g, :, q : q + cols] for q in range(3)]
        columns += [zq[g, :, q : q + cols] for q in range(2)]
    columns = [x.reshape(pairs * rows * cols * 16, 128) for x in columns]
    weight = weights[...].reshape(3 * 14 * 128, 256)
    return jnp.dot(jnp.concatenate(columns, 1), weight, preferred_element_type=F32)


def kernel(sizes, video_hbm, cin_hbm, cmid_hbm, gin_hbm, gmid_hbm, win_hbm, bin_hbm, wmid_hbm, bmid_hbm, out,
           gain_in, gain_mid, bias_in, bias_mid, video, cin, cmid, raw_in, raw_mid, w_in, w_mid, wide, mixed, order,
           oa, ob, corner, sa, sb, ma, mb, tile, side, angle, got_tile, got_row, got_side, got_angle,
           ta, zp, zq, ua, vp, vq, total_a, total_b,
           load_sem, send_sem, recv_sem, tile_sem):
    n_row, n_col = sizes
    slab, row, col = lax.axis_index("slab"), lax.axis_index("row"), lax.axis_index("col")
    loads = [pltpu.make_async_copy(src, dst, load_sem.at[n]) for n, (src, dst) in enumerate(
        [(video_hbm, video), (cin_hbm, cin), (cmid_hbm, cmid), (gin_hbm, gain_in), (gmid_hbm, gain_mid),
         (bin_hbm, bias_in), (bmid_hbm, bias_mid), (win_hbm, raw_in), (wmid_hbm, raw_mid)])]

    up, down, left, right = row > 0, row < n_row - 1, col > 0, col < n_col - 1
    there = [up, down, left, right, up & left, up & right, down & left, down & right]

    def device(s, dr, dc):
        return (s, lax.rem(row + dr + n_row, n_row), lax.rem(col + dc + n_col, n_col))

    barrier = pltpu.get_barrier_semaphore()
    for n in FAR_FIRST:
        @pl.when(there[n])
        def _():
            for s in range(2):
                pl.semaphore_signal(barrier, inc=1, device_id=device(s, *AROUND[n]), device_id_type=pl.DeviceIdType.MESH)
    pl.semaphore_signal(barrier, inc=1, device_id=(1 - slab, row, col), device_id_type=pl.DeviceIdType.MESH)
    n_up_down, n_sides = up.astype(jnp.int32) + down.astype(jnp.int32), left.astype(jnp.int32) + right.astype(jnp.int32)
    greetings = 2 * (n_up_down + n_sides + n_up_down * n_sides) + 1

    lanes8, lanes16 = low_lanes((8, 128)), low_lanes((16, 128))
    zero = jnp.zeros((1, 64), F32)

    def halves(ref):
        return ref[0:1, 0:128], jnp.concatenate([ref[0:1, 128:192], zero], 1)

    for load in loads:
        load.start()

    order_channels(order)
    for load in loads[:7]:
        load.wait()

    def columns_of(ref, f, j):
        return split_columns(*(ref[f, 3 * j + k].astype(F32) for k in range(3)), lanes8)

    def put_mixed(f, j, pixels):
        start = pl.multiple_of(f * 128 + j * 16, 16)
        mixed[0, pl.ds(start, 16), 0:128] = jnp.concatenate([pixels[0][0], pixels[1][0]], 0).astype(BF16)
        mixed[0, pl.ds(start, 16), 128:256] = jnp.concatenate([pixels[0][1], pixels[1][1]], 0).astype(BF16)

    gain_a, gain_b = halves(gain_in)

    def activate_frame(n, _):
        f = n
        for j in range(8):
            put_mixed(f, j, [act(a, b, gain_a, gain_b, lanes8) for a, b in columns_of(video, f, j)])
        return 0

    def mix_caches(j, _):
        for f in range(2):
            put_mixed(f, j, columns_of(cmid, f, j))
            put_mixed(2 + f, j, columns_of(cin, f, j))
        return 0

    def reorder():
        ordered = jnp.dot(mixed[0], order[...], preferred_element_type=F32)
        oa[...] = ordered[:, 0:128]
        ob[...] = ordered[:, 128:256]

    def line_of(o, f, i):
        return [o[pl.ds(f * 128 + h * 64 + i, 8, stride=8), :] for h in range(2)]

    def pack(k):
        def two_rows(n, _):
            f, u = n // 4, n % 4
            for r in range(2):
                tile[k, f, u, r] = jnp.concatenate(line_of(oa, f, 2 * u + r), 0).astype(BF16)
            b = [jnp.concatenate(line_of(ob, f, 2 * u + r), 0) for r in range(2)]
            tile[k, f, u, 2] = jnp.where(lanes16, b[0], b[1]).astype(BF16)
            return 0

        lax.fori_loop(0, 16, two_rows, 0, unroll=4)
        for v, j in enumerate((0, 14)):
            for f in range(4):
                side[k, v, f // 2, f % 2] = oa[pl.ds((f * 16 + j) * 8, 16), :].astype(BF16)
            for f in range(0, 4, 2):
                b = [ob[pl.ds(((f + e) * 16 + j) * 8, 16), :] for e in range(2)]
                side[k, v, f // 2, 2] = jnp.where(lanes16, b[0], b[1]).astype(BF16)
        for n, (i0, j0) in enumerate(((0, 0), (0, 14), (6, 0), (6, 14))):
            for h, o in enumerate((oa, ob)):
                for x in range(4):
                    at = (j0 + x % 2) * 8 + i0 + x // 2
                    corner[2 * n + h, 4 * x : 4 * x + 4, :] = o[pl.ds(at, 4, stride=128), :]
        for n in range(4):
            for h in range(2):
                angle[k, n, h] = corner[2 * n + h].astype(BF16)

    def messages(k, s, slot):
        sources = [tile.at[k, :, 0], tile.at[k, :, 3], side.at[k, 0], side.at[k, 1]] + [angle.at[k, n] for n in range(4)]
        targets = [got_row.at[slot, 1], got_row.at[slot, 0], got_side.at[slot, 1], got_side.at[slot, 0]]
        targets += [got_angle.at[slot, 3 - n] for n in range(4)]
        return [pltpu.make_async_remote_copy(
            src_ref=src, dst_ref=dst, send_sem=send_sem.at[slot, n], recv_sem=recv_sem.at[slot, n],
            device_id=device(s, dr, dc), device_id_type=pl.DeviceIdType.MESH)
            for n, (src, dst, (dr, dc)) in enumerate(zip(sources, targets, AROUND))]

    def each(copies, method, condition=None):
        exist = [there[n] for n in (1, 0, 3, 2, 7, 6, 5, 4)] if method == "wait_recv" else there
        for copy, has in [(copies[n], exist[n]) for n in FAR_FIRST]:
            @pl.when(has if condition is None else has & condition)
            def _():
                getattr(copy, method)()

    own = messages(0, slab, 1)
    early_frames = messages(0, 1, 0)
    early_caches = messages(1, 0, 0)
    to_partner = pltpu.make_async_remote_copy(
        src_ref=tile.at[0], dst_ref=got_tile, send_sem=tile_sem.at[0], recv_sem=tile_sem.at[1],
        device_id=(1 - slab, row, col), device_id_type=pl.DeviceIdType.MESH)

    def place_tile(f0):
        def one(f, i, line, r):
            at = ((f0 + f) * 13 + line + PAD) * LINE + r * HALF + 2
            for o, s in ((oa, sa), (ob, sb)):
                for h, x in enumerate(line_of(o, f, i)):
                    s[pl.ds(at + 8 * h, 8), :] = x

        def frame(f, _):
            for i in range(8):
                if i < 5:
                    one(f, i, i + 2, 0)
                if i > 2:
                    one(f, i, i - 3, 1)
            return 0

        lax.fori_loop(0, 4, frame, 0)

    lax.fori_loop(0, 4, activate_frame, 0)
    reorder()
    pack(0)
    pl.semaphore_wait(barrier, greetings)
    @pl.when(slab == 0)
    def _():
        to_partner.start()

    each(early_frames, "start", slab == 0)
    each(own, "start")

    place_tile(4)
    lax.fori_loop(0, 8, mix_caches, 0, unroll=4)
    reorder()

    @pl.when(slab == 1)
    def _():
        pack(1)

    each(early_caches, "start", slab == 1)

    @pl.when(slab == 0)
    def _():
        place_tile(0)

    for w in (w_in, w_mid):
        w[:, 13 * 128 : 13 * 128 + 64, :] = jnp.zeros((3, 64, 256), BF16)
    loads[7].wait()

    def lay_out_all(raw, out):
        def part(n, _):
            lay_out_weights(raw, wide, out, n // 3, n % 3)
            return 0

        lax.fori_loop(0, 9, part, 0)

    lay_out_all(raw_in, w_in)
    loads[8].wait()
    lay_out_all(raw_mid, w_mid)

    def clear(x, has):
        return jnp.where(has, x, 0.0)

    def unmerge(b):
        other = swap(b)
        return jnp.where(lanes16, b, other), jnp.where(lanes16, other, b)

    def place_rows(slot):
        for v, has in enumerate((up, down)):
            line, r = ((0, 0), (5, 1))[v]

            def frame(f, _):
                at = ((slot * 4 + f) * 13 + line + PAD) * LINE + r * HALF + 2
                b = unmerge(clear(got_row[slot, v, f, 2].astype(F32), has))
                for n in range(2):
                    sa[pl.ds(at + n * LINE, 16), :] = clear(got_row[slot, v, f, n].astype(F32), has)
                    sb[pl.ds(at + n * LINE, 16), :] = b[n]
                return 0

            lax.fori_loop(0, 4, frame, 0, unroll=True)

    def put_columns(s, f, j, x):
        for n in range(2):
            at = f * IMAGE + j + n
            s[pl.ds(at + (2 + PAD) * LINE, 8, stride=LINE), :] = x[8 * n : 8 * n + 8]
            s[pl.ds(at + (PAD - 3) * LINE + HALF, 8, stride=LINE), :] = x[8 * n : 8 * n + 8]

    def place_sides(slot):
        for v, has in enumerate((left, right)):
            for pair in range(2):
                b = unmerge(clear(got_side[slot, v, pair, 2].astype(F32), has))
                for e in range(2):
                    f = slot * 4 + pair * 2 + e
                    put_columns(sa, f, 18 * v, clear(got_side[slot, v, pair, e].astype(F32), has))
                    put_columns(sb, f, 18 * v, b[e])

    def place_angles(slot):
        for n, has in enumerate(there[4:]):
            for h, s in enumerate((sa, sb)):
                corner[2 * n + h] = clear(got_angle[slot, n, h].astype(F32), has)
        for n in range(4):
            line, r = ((0, 0), (5, 1))[n // 2]
            for h, s in enumerate((sa, sb)):
                for x in range(4):
                    at = slot * 4 * IMAGE + (line + x // 2 + PAD) * LINE + r * HALF + 18 * (n % 2) + x % 2
                    s[pl.ds(at, 4, stride=IMAGE), :] = corner[2 * n + h, 4 * x : 4 * x + 4, :]

    def unpack_tile():
        def frame(f, _):
            for u in range(4):
                b = unmerge(got_tile[f, u, 2].astype(F32))
                for n in range(2):
                    i = 2 * u + n
                    a = got_tile[f, u, n].astype(F32)
                    for line, r, fits in ((i + 2, 0, i < 5), (i - 3, 1, i > 2)):
                        if fits:
                            at = (f * 13 + line + PAD) * LINE + r * HALF + 2
                            sa[pl.ds(at, 16), :] = a
                            sb[pl.ds(at, 16), :] = b[n]
            return 0

        lax.fori_loop(0, 4, frame, 0)

    @pl.when(slab == 1)
    def _():
        to_partner.wait_recv()
        unpack_tile()

    each(own, "wait_recv")
    for slot in (1, 0):
        if slot == 0:
            each(early_frames, "wait_recv")
        place_rows(slot)
        place_sides(slot)
        place_angles(slot)

    def start_in(g, i, j):
        return (g * 13 + i + PAD) * LINE + j

    gather_taps(sa, sb, ta, zp, zq, start_in, 5, 1, 2 - 2 * slab, 7, 7, 7)
    bias_a, bias_b = halves(bias_in)
    gain_a, gain_b = halves(gain_mid)
    subs = lax.broadcasted_iota(jnp.int32, (16, 128), 0) & 7

    def middle_pair(k, _):
        result = convolve(ta, zp, zq, w_in, 2 * k, 1, 5, 5)
        total_a[k, 0:400] = result[:, 0:128]
        total_b[k, 0:400] = result[:, 128:256]
        for i in range(5):
            for j in range(5):
                at = (i * 5 + j) * 16
                ya, yb = act(
                    total_a[k, at : at + 16, :] + bias_a, total_b[k, at : at + 16, :] + bias_b, gain_a, gain_b, lanes16)
                gone = []
                if i == 0:
                    gone.append(jnp.logical_not(up) & (subs < 4))
                if i == 4:
                    gone.append(jnp.logical_not(down) & (subs >= 4))
                if j == 0:
                    gone.append(jnp.logical_not(left) & ((subs & 3) == 0))
                if j == 2:
                    gone.append(jnp.logical_not(right) & ((subs & 3) == 3))
                if gone:
                    gone = functools.reduce(jnp.logical_or, gone)
                    ya, yb = jnp.where(gone, 0.0, ya), jnp.where(gone, 0.0, yb)
                mixed[k, at : at + 16, 0:128] = ya.astype(BF16)
                mixed[k, at : at + 16, 128:256] = yb.astype(BF16)
        ordered = jnp.dot(mixed[k, 0:400], order[...], preferred_element_type=F32)
        for n in range(25):
            for h in range(2):
                at = (2 * k + h) * MIDDLE + (n // 5) * LINE + n % 5
                y = ordered[n * 16 + 8 * h : n * 16 + 8 * h + 8]
                ma[pl.ds(at, 8, stride=5), :] = y[:, 0:128]
                mb[pl.ds(at, 8, stride=5), :] = y[:, 128:256]
        return 0

    lax.fori_loop(1 - slab, 3, middle_pair, 0)

    @pl.when(slab == 0)
    def _():
        def frame(f, _):
            for n in range(10):
                line, r = (n + 1, 0) if n < 6 else (n - 4, 1)
                source = (f * 13 + line + PAD) * LINE + r * HALF + 1
                at = f * MIDDLE + (n % 5) * LINE + (n // 5) * HALF
                for s, m in ((sa, ma), (sb, mb)):
                    m[pl.ds(at, 16), :] = s[pl.ds(source, 16), :]
                    m[pl.ds(at + 16, 2), :] = s[pl.ds(source + 16, 2), :]
            return 0

        lax.fori_loop(0, 2, frame, 0)

    def start_mid(g, i, j):
        return g * MIDDLE + (i % 5) * LINE + (i // 5) * HALF + j

    gather_taps(ma, mb, ua, vp, vq, start_mid, 2, 2, 0, 4, 10, 4)
    bias_a, bias_b = halves(bias_mid)

    def result_pair(k):
        result = convolve(ua, vp, vq, w_mid, k, 1, 8, 2)
        total_a[k, 0:256] = result[:, 0:128]
        total_b[k, 0:256] = result[:, 128:256]
        for h in range(2):
            f = k + 2 * h
            for c in range(8):
                at = h * 8 + c
                ae = total_a[k, pl.ds(at, 8, stride=32), :] + bias_a
                be = total_b[k, pl.ds(at, 8, stride=32), :] + bias_b
                ao = swap(total_a[k, pl.ds(at + 16, 8, stride=32), :] + bias_a)
                bo = swap(total_b[k, pl.ds(at + 16, 8, stride=32), :] + bias_b)
                for n, branch in enumerate((ae, jnp.where(lanes8, be, ao), jnp.where(lanes8, ao, bo))):
                    out[f, 3 * c + n] = (video[f, 3 * c + n].astype(F32) + branch).astype(BF16)

    for k in range(2):
        result_pair(k)

    each(own, "wait_send")
    each(early_frames, "wait_send", slab == 0)
    each(early_caches, "wait_send", slab == 1)

    @pl.when(slab == 0)
    def _():
        to_partner.wait_send()


def body(sizes, video, cache_in, cache_mid, gain_in, gain_mid, conv_in, bias_in, conv_mid, bias_mid):
    def tiles(x):
        return x.reshape(x.shape[0], 8, 24, 128).transpose(0, 2, 1, 3)

    def taps(x):
        return x.reshape(3, 3, 864, 128).transpose(0, 2, 1, 3)

    def line(x):
        return x.reshape(1, CHAN)

    hbm, vmem = pl.BlockSpec(memory_space=pltpu.HBM), pl.BlockSpec(memory_space=pltpu.VMEM)
    scratch = [
        pltpu.VMEM((1, CHAN), F32),
        pltpu.VMEM((1, CHAN), F32),
        pltpu.VMEM((1, CHAN), F32),
        pltpu.VMEM((1, CHAN), F32),
        pltpu.VMEM((4, 24, 8, 128), BF16),
        pltpu.VMEM((2, 24, 8, 128), BF16),
        pltpu.VMEM((2, 24, 8, 128), BF16),
        pltpu.VMEM((3, 864, 3, 128), BF16),
        pltpu.VMEM((3, 864, 3, 128), BF16),
        pltpu.VMEM((3, 14 * 128, 256), BF16),
        pltpu.VMEM((3, 14 * 128, 256), BF16),
        pltpu.VMEM((12 * 24, 8, 128), F32),
        pltpu.VMEM((3, 512, 256), BF16),
        pltpu.VMEM((256, 256), BF16),
        pltpu.VMEM((512, 128), F32),
        pltpu.VMEM((512, 128), F32),
        pltpu.VMEM((8, 16, 128), F32),
        pltpu.VMEM((8 * IMAGE, 128), F32),
        pltpu.VMEM((8 * IMAGE, 128), F32),
        pltpu.VMEM((6 * MIDDLE, 128), F32),
        pltpu.VMEM((6 * MIDDLE, 128), F32),
        pltpu.VMEM((2, 4, 4, 3, 16, 128), BF16),
        pltpu.VMEM((2, 2, 2, 3, 16, 128), BF16),
        pltpu.VMEM((2, 4, 2, 16, 128), BF16),
        pltpu.VMEM((4, 4, 3, 16, 128), BF16),
        pltpu.VMEM((2, 2, 4, 3, 16, 128), BF16),
        pltpu.VMEM((2, 2, 2, 3, 16, 128), BF16),
        pltpu.VMEM((2, 4, 2, 16, 128), BF16),
        pltpu.VMEM((7, 7, 7, 16, 128), BF16),
        pltpu.VMEM((7, 5, 7, 16, 128), BF16),
        pltpu.VMEM((7, 5, 6, 16, 128), BF16),
        pltpu.VMEM((4, 10, 4, 16, 128), BF16),
        pltpu.VMEM((4, 8, 4, 16, 128), BF16),
        pltpu.VMEM((4, 8, 3, 16, 128), BF16),
        pltpu.VMEM((3, 400, 128), F32),
        pltpu.VMEM((3, 400, 128), F32),
        pltpu.SemaphoreType.DMA((9,)),
        pltpu.SemaphoreType.DMA((2, 8)),
        pltpu.SemaphoreType.DMA((2, 8)),
        pltpu.SemaphoreType.DMA((2,)),
    ]
    result = pl.pallas_call(
        functools.partial(kernel, sizes),
        out_shape=jax.ShapeDtypeStruct((4, 24, 8, 128), BF16),
        in_specs=[hbm] * 9,
        out_specs=vmem,
        scratch_shapes=scratch,
        compiler_params=pltpu.CompilerParams(
            collective_id=0, has_side_effects=True, vmem_limit_bytes=52 << 20),
        cost_estimate=pl.CostEstimate(flops=3_000_000_000, bytes_accessed=6_000_000, transcendentals=300_000),
    )(*(pltpu.with_memory_space_constraint(x, pltpu.HBM) for x in (
        tiles(video), tiles(cache_in), tiles(cache_mid), line(gain_in), line(gain_mid),
        taps(conv_in), line(bias_in), taps(conv_mid), line(bias_mid))))
    return result.transpose(0, 2, 1, 3).reshape(video.shape)


def solution(mesh):
    tile = P("slab", "row", "col")
    cache = P(None, "row", "col")
    sizes = (mesh.shape["row"], mesh.shape["col"])
    return jax.shard_map(
        functools.partial(body, sizes), mesh=mesh,
        in_specs=(tile, cache, cache, P(), P(), P(), P(), P(), P()),
        out_specs=tile, check_vma=False)
```
